32 devices in a mesh: geom: 2 (over x), aux: 16 (over z, y, core).
Axes of the slice: x: 2, y: 2, z: 4, core: 2. Of those that a mesh axis runs over, the one named last changes fastest.
Arguments:
- trial_vecs: float32 [8, 128, 224], P('geom', 'aux'), parts along dimension 0, may hold values from -6 to 6
- occ_energy: float32 [256], P('geom'), parts along dimension 0, may hold values from -1.5 to -0.2
- vir_energy: float32 [448], P('geom'), parts along dimension 0, may hold values from 0.2 to 2.5
- coul_ov: bfloat16 [2048, 128, 224], P(('geom', 'aux')), parts along dimension 0, may hold values from -0.03125 to 0.03125
- exch_oo: bfloat16 [2048, 128, 128], P(('geom', 'aux')), parts along dimension 0, may hold values from -0.0234375 to 0.0234375
- exch_vv: bfloat16 [2048, 224, 224], P(('geom', 'aux')), parts along dimension 0, may hold values from -0.375 to 0.375
Outputs:
- sigma_vecs: float32 [8, 128, 224], P('geom', 'aux'), parts along dimension 0
- update_vecs: float32 [8, 128, 224], P('geom', 'aux'), parts along dimension 0
The draws below stay inside these ranges and needn't reach their ends.
There are 2 independent parts, one for each index of `geom`. The reference program is written for one: setup_inputs(seed, part) draws one part's arguments, and reference() takes and returns one part's arrays. A program takes and returns all parts, laid end to end along the dimension named above; each array names one. Nothing has to cross between parts.
All inputs are finite; a program needn't handle non-finite values.
Results may differ from the reference program's by a relative error of at most 0.0037.
Values may be sent and summed in bfloat16 or wider, within the bound.
A program may use at most 64 MiB of HBM per device.

```python
import jax
import jax.numpy as jnp
from jax import lax

NT = 4
NO = 128
VB = 224
AUX_DEV = 64
NAUX = 1024
N_AUX = 16


def strengthened(array, rng, source, target, blocks, factor):
    def block_of(axis_at):
        return (jnp.arange(array.shape[axis_at]) // (array.shape[axis_at] // blocks)).reshape((-1,) + (1,) * (array.ndim - 1 - axis_at))

    first = jax.random.permutation(rng, blocks)[block_of(target)]
    second = (block_of(target) + blocks // 2) % blocks
    return jnp.where((block_of(source) == first) | (block_of(source) == second), factor * array, array)


def level_of(key, extent, cuts, low, top_value):
    gain, own = 1.0, jax.random.fold_in(key, 6)
    for axis_at, blocks in cuts:
        heights = jnp.exp(jax.random.uniform(jax.random.fold_in(own, axis_at), (blocks,), jnp.float32, low / len(cuts), top_value / len(cuts)))
        gain = gain * jnp.repeat(heights, extent[axis_at] // blocks).reshape([-1 if axis == axis_at else 1 for axis in range(len(extent))])
    return gain


def gaussian(stream_key, dims, deviation, bound, shards=(), dtype=jnp.bfloat16):
    drawn = jax.random.normal(stream_key, dims, jnp.float32) * deviation
    if len(shards) > 0:
        drawn = level_of(stream_key, dims, shards, -0.22, 0.18) * drawn
    return jnp.clip(drawn, min=-bound, max=bound).astype(dtype)


def gaussian_with(rng, shape, deviation, most, shards, heavy, kind=jnp.bfloat16):
    drawn = deviation * jax.random.normal(rng, shape, jnp.float32)
    if shards:
        drawn = drawn * level_of(rng, shape, shards, -0.22, 0.18)
    return jnp.clip(strengthened(drawn, jax.random.fold_in(rng, 3), *heavy), -most, most).astype(kind)


def setup_inputs(seed: int = 0, part: int = 0) -> dict:
    keys = jax.random.split(jax.random.key(seed), 7)
    part_keys = jax.random.split(jax.random.fold_in(keys[6], part), 7)
    trial_vecs = gaussian(part_keys[0], (NT, NO, VB), 1.0, 6.0, ((1, 16),), jnp.float32)
    occ_energy = jnp.clip(jax.random.uniform(part_keys[1], (NO,), jnp.float32, -1.5, -0.2), -1.5, -0.2)
    vir_energy = jnp.clip(jax.random.uniform(part_keys[2], (VB,), jnp.float32, 0.2, 2.5), 0.2, 2.5)
    coul_ov = gaussian(part_keys[3], (NAUX, NO, VB), (NO * VB) ** -0.5, 0.03125, ((0, 16),))
    exch_oo = gaussian_with(part_keys[4], (NAUX, NO, NO), (AUX_DEV * N_AUX * NO) ** -0.5, 0.0234375, ((0, 16),), (0, 1, 16, 2.0))
    exch_vv = gaussian(part_keys[5], (NAUX, VB, VB), VB ** -0.5, 0.375, ((0, 16),))
    return {"trial_vecs": trial_vecs, "occ_energy": occ_energy, "vir_energy": vir_energy, "coul_ov": coul_ov, "exch_oo": exch_oo, "exch_vv": exch_vv}


def reference(trial_vecs, occ_energy, vir_energy, coul_ov, exch_oo, exch_vv):
    rounded = trial_vecs.astype(jnp.bfloat16)
    wide_x = rounded.astype(jnp.float32)
    n_trial = trial_vecs.shape[0]
    n_occ = trial_vecs.shape[1]
    n_virt = trial_vecs.shape[2]
    ov_blocks = coul_ov.reshape(N_AUX, AUX_DEV, n_occ, n_virt)
    oo_blocks = exch_oo.reshape(N_AUX, AUX_DEV, n_occ, n_occ)
    vv_blocks = exch_vv.reshape(N_AUX, AUX_DEV, n_virt, n_virt)

    def advance(totals, parts):
        ov_part, oo_part, vv_part = parts
        ov_wide = ov_part.astype(jnp.float32)
        aux_coef = jnp.einsum('pia,nia->np', ov_wide, wide_x)
        coef_low = lax.optimization_barrier(aux_coef.astype(jnp.bfloat16))
        coulomb = jnp.einsum('pia,np->nia', ov_wide, coef_low.astype(jnp.float32))
        halfway = jnp.einsum('pab,njb->pnja', vv_part.astype(jnp.float32), wide_x)
        halfway = lax.optimization_barrier(halfway.astype(jnp.bfloat16))
        exchange = jnp.einsum('pij,pnja->nia', oo_part.astype(jnp.float32), halfway.astype(jnp.float32))
        return ((totals[0] + coulomb, totals[1] + exchange), None)
    empty = jnp.zeros((n_trial, n_occ, n_virt), jnp.float32)
    sums, _ = lax.scan(advance, (empty, empty), (ov_blocks, oo_blocks, vv_blocks))
    diagonal = vir_energy[None, :] - occ_energy[:, None]
    sigma_vecs = diagonal[None] * trial_vecs + 2.0 * sums[0] - sums[1]
    omega = lax.optimization_barrier(jnp.sum(trial_vecs * sigma_vecs, axis=(1, 2))) / (lax.optimization_barrier(jnp.sum(trial_vecs * trial_vecs, axis=(1, 2))) + 1e-06)
    resid = sigma_vecs - omega[:, None, None] * trial_vecs
    gap = jnp.maximum(jnp.abs(diagonal[None] - omega[:, None, None]), 1.0)
    precond = resid / gap
    update_vecs = precond * lax.rsqrt(lax.optimization_barrier(jnp.mean(precond * precond, axis=(1, 2))) + 1e-06)[:, None, None]
    return (sigma_vecs, update_vecs)
```

```python
import functools
import math

import jax
import jax.numpy as jnp
from jax import lax
from jax.experimental import pallas as pl
from jax.experimental.pallas import tpu as pltpu
from jax.sharding import PartitionSpec as P

MESH = pl.DeviceIdType.MESH
NT_DIMS = (((1,), (1,)), ((), ()))


def sigma_kernel(
    n_dev,
    group,
    x_ref,
    occ_ref,
    vir_ref,
    coul_hbm,
    oo_hbm,
    vv_hbm,
    sigma_ref,
    update_ref,
    coul,
    oo,
    vv,
    x_pad,
    gathered,
    x_t,
    total,
    outgoing,
    incoming,
    scalars_out,
    scalars_in,
    norms_out,
    norms_in,
    load_sem,
    gather_send,
    gather_recv,
    sum_send,
    sum_recv,
    scalar_send,
    scalar_recv,
    norm_send,
    norm_recv,
):
    me = lax.axis_index("aux")
    n_trial, rows, n_virt = x_ref.shape
    aux_local, n_occ, _ = oo.shape
    width = x_pad.shape[1]
    half_trials = n_trial // 2
    half_cols = half_trials * n_occ
    f32, bf16 = jnp.float32, jnp.bfloat16

    loads = [
        pltpu.make_async_copy(source, target, load_sem.at[slot])
        for slot, (source, target) in enumerate(((coul_hbm, coul), (vv_hbm, vv), (oo_hbm, oo)))
    ]
    for load in loads:
        load.start()

    barrier = pltpu.get_barrier_semaphore()

    def greet(step, carry):
        pl.semaphore_signal(
            barrier, inc=1, device_id={"aux": lax.rem(me + step, n_dev)}, device_id_type=MESH
        )
        return carry

    lax.fori_loop(1, n_dev, greet, 0)

    x_pad[...] = jnp.zeros_like(x_pad)
    x_pad[:, :n_virt] = x_ref[...].reshape(n_trial * rows, n_virt)
    gathered[me] = x_pad[...].astype(bf16)
    pl.semaphore_wait(barrier, n_dev - 1)

    def to_peer(source, target, send_sem, recv_sem, step):
        return pltpu.make_async_remote_copy(
            src_ref=source,
            dst_ref=target,
            send_sem=send_sem.at[step],
            recv_sem=recv_sem.at[step],
            device_id={"aux": lax.rem(me + step, n_dev)},
            device_id_type=MESH,
        )

    def gather_copy(step):
        return to_peer(gathered.at[me], gathered.at[me], gather_send, gather_recv, step)

    def sum_copy(half, step):
        peer = lax.rem(me + step, n_dev)
        return to_peer(
            outgoing.at[half, peer], incoming.at[half, me], sum_send.at[half], sum_recv.at[half], step
        )

    def scalar_copy(step):
        return to_peer(scalars_out, scalars_in.at[me], scalar_send, scalar_recv, step)

    def norm_copy(step):
        return to_peer(norms_out, norms_in.at[me], norm_send, norm_recv, step)

    def each(action):
        def body(step, carry):
            action(step)
            return carry

        lax.fori_loop(1, n_dev, body, 0)

    each(lambda step: gather_copy(step).start())
    for load in loads:
        load.wait()
    each(lambda step: gather_copy(step).wait_recv())

    wide = gathered[...].astype(f32).reshape(n_dev, n_trial, rows, width)
    for n in range(n_trial):
        x_t[:, n * n_occ : (n + 1) * n_occ] = (
            wide[:, n].reshape(n_occ, width).T.astype(bf16)
        )

    block = 16
    pairs = n_virt // (2 * block)
    z_rows, z_cols = n_trial * block, aux_local * block

    def coul_block(pair):
        return jnp.concatenate(
            [
                coul[:, (2 * pair + t) * block : (2 * pair + t + 1) * block, :].reshape(z_cols, n_occ)
                for t in range(2)
            ],
            axis=1,
        )

    z = jnp.zeros((z_rows, z_cols), f32)
    for pair in range(pairs):
        left = jnp.concatenate(
            [
                jnp.concatenate(
                    [
                        x_t[
                            (2 * pair + t) * block : (2 * pair + t + 1) * block,
                            n * n_occ : (n + 1) * n_occ,
                        ]
                        for n in range(n_trial)
                    ],
                    axis=0,
                )
                for t in range(2)
            ],
            axis=1,
        )
        z = z + lax.dot_general(left, coul_block(pair), NT_DIMS, preferred_element_type=f32)
    same = (
        lax.broadcasted_iota(jnp.int32, (z_rows, z_cols), 0) % block
        == lax.broadcasted_iota(jnp.int32, (z_rows, z_cols), 1) % block
    )
    z = jnp.where(same, z, 0.0).reshape(n_trial, block, z_cols)
    z = jnp.broadcast_to(jnp.sum(z, axis=1, keepdims=True), (n_trial, block, z_cols))
    z = z.reshape(z_rows, z_cols)
    lanes = 128
    ones = (
        lax.broadcasted_iota(jnp.int32, (lanes, lanes), 0) // block
        == lax.broadcasted_iota(jnp.int32, (lanes, lanes), 1) // block
    ).astype(f32)
    coef = jnp.concatenate(
        [
            jnp.dot(
                z[:, c * lanes : (c + 1) * lanes],
                ones,
                precision=lax.Precision.HIGHEST,
                preferred_element_type=f32,
            )
            for c in range(z_cols // lanes)
        ],
        axis=1,
    )
    spread = jnp.where(same, coef, 0.0).astype(bf16)
    total[...] = jnp.zeros_like(total)
    for pair in range(pairs):
        part = 2.0 * jnp.dot(spread, coul_block(pair), preferred_element_type=f32)
        for t in range(2):
            for n in range(n_trial):
                total[n, (2 * pair + t) * block : (2 * pair + t + 1) * block, :] = part[
                    n * block : (n + 1) * block, t * n_occ : (t + 1) * n_occ
                ]

    for half in range(2):
        x_half = x_t[:n_virt, half * half_cols : (half + 1) * half_cols]

        def exchange(index, carry, half=half, x_half=x_half):
            first = index * group
            halfway = jnp.dot(
                vv[pl.ds(first, group)].reshape(group * n_virt, n_virt),
                x_half,
                preferred_element_type=f32,
            ).astype(bf16)
            left = jnp.concatenate(
                [
                    jnp.concatenate(
                        [
                            halfway[p * n_virt : (p + 1) * n_virt, n * n_occ : (n + 1) * n_occ]
                            for p in range(group)
                        ],
                        axis=1,
                    )
                    for n in range(half_trials)
                ],
                axis=0,
            )
            right = jnp.concatenate([oo[first + p] for p in range(group)], axis=1)
            part = lax.dot_general(left, right, NT_DIMS, preferred_element_type=f32)
            for n in range(half_trials):
                at = half * half_trials + n
                total[at, :n_virt, :] = (
                    total[at, :n_virt, :] - part[n * n_virt : (n + 1) * n_virt, :]
                )
            return carry

        lax.fori_loop(0, aux_local // group, exchange, 0)
        outgoing[half] = jnp.concatenate(
            [
                total[half * half_trials + n].T.reshape(n_dev, rows, width)
                for n in range(half_trials)
            ],
            axis=1,
        ).astype(bf16)
        each(lambda step, half=half: sum_copy(half, step).start())
        incoming[half, me] = outgoing[half, me]

    row_at = lax.broadcasted_iota(jnp.int32, (rows, n_occ), 0) + me * rows
    col_at = lax.broadcasted_iota(jnp.int32, (rows, n_occ), 1)
    occ_rows = jnp.sum(jnp.where(row_at == col_at, occ_ref[...], 0.0), axis=1, keepdims=True)
    diagonal = vir_ref[...] - occ_rows

    def whole(value):
        return jnp.sum(jnp.sum(value, axis=0, keepdims=True), axis=1, keepdims=True)

    numer, denom = [], []
    for n in range(n_trial):
        own = x_ref[n]
        square = own * own
        x_n = x_t[:, n * n_occ : (n + 1) * n_occ].astype(f32)
        numer.append(whole(x_n * total[n]) + whole(diagonal * square))
        denom.append(whole(square))
    for n in range(n_trial):
        scalars_out[n : n + 1, :] = jnp.broadcast_to(numer[n], (1, lanes))
        scalars_out[n_trial + n : n_trial + n + 1, :] = jnp.broadcast_to(denom[n], (1, lanes))
    each(lambda step: scalar_copy(step).start())
    scalars_in[me] = scalars_out[...]

    for half in range(2):
        each(lambda step, half=half: sum_copy(half, step).wait_recv())
    each(lambda step: scalar_copy(step).wait_recv())

    sums = jnp.sum(scalars_in[...], axis=0)
    precond = []
    for n in range(n_trial):
        if n % half_trials == 0:
            summed = jnp.sum(incoming[n // half_trials].astype(f32), axis=0)
        at = (n % half_trials) * rows
        own = x_ref[n]
        sigma = diagonal * own + summed[at : at + rows, :n_virt]
        sigma_ref[n] = sigma
        omega = sums[n : n + 1, :1] / (sums[n_trial + n : n_trial + n + 1, :1] + 1e-06)
        resid = sigma - omega * own
        precond.append(resid / jnp.maximum(jnp.abs(diagonal - omega), 1.0))
        norms_out[n : n + 1, :] = jnp.broadcast_to(whole(precond[n] * precond[n]), (1, lanes))
    each(lambda step: norm_copy(step).start())
    norms_in[me] = norms_out[...]
    each(lambda step: norm_copy(step).wait_recv())
    norms = jnp.sum(norms_in[...], axis=0)
    count = float(n_occ * n_virt)
    for n in range(n_trial):
        update_ref[n] = precond[n] * lax.rsqrt(norms[n : n + 1, :1] / count + 1e-06)

    each(lambda step: gather_copy(step).wait_send())
    for half in range(2):
        each(lambda step, half=half: sum_copy(half, step).wait_send())
    each(lambda step: scalar_copy(step).wait_send())
    each(lambda step: norm_copy(step).wait_send())


def on_device(n_dev, trial_vecs, occ_energy, vir_energy, coul_ov, exch_oo, exch_vv):
    n_trial, rows, n_virt = trial_vecs.shape
    aux_local, n_occ, _ = exch_oo.shape
    width = -(-n_virt // 128) * 128
    half_rows = n_trial // 2 * rows
    vmem = pl.BlockSpec(memory_space=pltpu.VMEM)
    anywhere = pl.BlockSpec(memory_space=pl.ANY)
    out = jax.ShapeDtypeStruct(trial_vecs.shape, jnp.float32)
    dma = pltpu.SemaphoreType.DMA
    return pl.pallas_call(
        functools.partial(sigma_kernel, n_dev, math.gcd(aux_local, 4)),
        out_shape=(out, out),
        in_specs=[vmem] * 3 + [anywhere] * 3,
        out_specs=(vmem, vmem),
        scratch_shapes=[
            pltpu.VMEM((aux_local, n_virt, n_occ), jnp.bfloat16),
            pltpu.VMEM((aux_local, n_occ, n_occ), jnp.bfloat16),
            pltpu.VMEM((aux_local, n_virt, n_virt), jnp.bfloat16),
            pltpu.VMEM((n_trial * rows, width), jnp.float32),
            pltpu.VMEM((n_dev, n_trial * rows, width), jnp.bfloat16),
            pltpu.VMEM((width, n_trial * n_occ), jnp.bfloat16),
            pltpu.VMEM((n_trial, width, n_occ), jnp.float32),
            pltpu.VMEM((2, n_dev, half_rows, width), jnp.bfloat16),
            pltpu.VMEM((2, n_dev, half_rows, width), jnp.bfloat16),
            pltpu.VMEM((2 * n_trial, 128), jnp.float32),
            pltpu.VMEM((n_dev, 2 * n_trial, 128), jnp.float32),
            pltpu.VMEM((2 * n_trial, 128), jnp.float32),
            pltpu.VMEM((n_dev, 2 * n_trial, 128), jnp.float32),
            dma((3,)),
            dma((n_dev,)),
            dma((n_dev,)),
            dma((2, n_dev)),
            dma((2, n_dev)),
            dma((n_dev,)),
            dma((n_dev,)),
            dma((n_dev,)),
            dma((n_dev,)),
        ],
        compiler_params=pltpu.CompilerParams(
            collective_id=0, has_side_effects=True, vmem_limit_bytes=56 * 1024 * 1024
        ),
    )(
        trial_vecs,
        occ_energy[None, :],
        vir_energy[None, :],
        coul_ov.transpose(0, 2, 1),
        exch_oo,
        exch_vv,
    )


def contract(rows_x, coul_ov, exch_oo, exch_vv):
    aux_coef = jnp.einsum("pia,nia->np", coul_ov, rows_x, preferred_element_type=jnp.float32)
    coulomb = jnp.einsum(
        "pia,np->nia", coul_ov, aux_coef.astype(jnp.bfloat16), preferred_element_type=jnp.float32
    )
    aux_local, n_occ, _ = exch_oo.shape
    n_virt = exch_vv.shape[1]
    group_size = math.gcd(aux_local, 16)
    vv_groups = exch_vv.reshape(aux_local // group_size, group_size, n_virt, n_virt)
    oo_groups = exch_oo.reshape(aux_local // group_size, group_size, n_occ, n_occ)

    def advance(running, parts_pair):
        vv_part, oo_part = parts_pair
        halfway = jnp.einsum(
            "pab,njb->pnja", vv_part, rows_x, preferred_element_type=jnp.float32
        ).astype(jnp.bfloat16)
        return (
            running
            + jnp.einsum("pij,pnja->nia", oo_part, halfway, preferred_element_type=jnp.float32),
            None,
        )

    exchange, _ = lax.scan(advance, jnp.zeros(rows_x.shape, jnp.float32), (vv_groups, oo_groups))
    return 2.0 * coulomb - exchange


def on_device_plain(trial_vecs, occ_energy, vir_energy, coul_ov, exch_oo, exch_vv):
    local_rows = trial_vecs.shape[1]
    n_occ, n_virt = coul_ov.shape[1:]
    row_start = lax.axis_index("aux") * local_rows
    rows_x = lax.all_gather(trial_vecs.astype(jnp.bfloat16), "aux", axis=1, tiled=True)
    summed = lax.psum_scatter(
        contract(rows_x, coul_ov, exch_oo, exch_vv), "aux", scatter_dimension=1, tiled=True
    )
    occ_rows = lax.dynamic_slice_in_dim(occ_energy, row_start, local_rows, 0)
    diagonal = vir_energy[None, :] - occ_rows[:, None]
    sigma = diagonal[None] * trial_vecs + summed
    sums = lax.psum(
        jnp.stack([jnp.sum(trial_vecs * sigma, (1, 2)), jnp.sum(trial_vecs * trial_vecs, (1, 2))]),
        "aux",
    )
    omega = (sums[0] / (sums[1] + 1e-06))[:, None, None]
    precond = (sigma - omega * trial_vecs) / jnp.maximum(jnp.abs(diagonal[None] - omega), 1.0)
    squares = lax.psum(jnp.sum(precond * precond, axis=(1, 2)), "aux") / (n_occ * n_virt)
    return sigma, precond * lax.rsqrt(squares + 1e-06)[:, None, None]


def solution(mesh):
    n_dev = mesh.shape["aux"]

    def body(trial_vecs, occ_energy, vir_energy, coul_ov, exch_oo, exch_vv):
        n_trial, rows, n_virt = trial_vecs.shape
        aux_local, n_occ, _ = exch_oo.shape
        tiled = (
            n_trial % 4 == 0
            and rows % 8 == 0
            and n_occ % 128 == 0
            and n_virt % 32 == 0
            and aux_local % 8 == 0
        )
        args = (trial_vecs, occ_energy, vir_energy, coul_ov, exch_oo, exch_vv)
        return on_device(n_dev, *args) if tiled else on_device_plain(*args)

    in_specs = (
        P("geom", "aux", None),
        P("geom"),
        P("geom"),
        P(("geom", "aux"), None, None),
        P(("geom", "aux"), None, None),
        P(("geom", "aux"), None, None),
    )
    out_specs = (P("geom", "aux", None), P("geom", "aux", None))
    return jax.shard_map(body, mesh=mesh, in_specs=in_specs, out_specs=out_specs, check_vma=False)
```

```python
import functools
import math

import jax
import jax.numpy as jnp
from jax import lax
from jax.experimental import pallas as pl
from jax.experimental.pallas import tpu as pltpu
from jax.sharding import PartitionSpec as P

MESH = pl.DeviceIdType.MESH
NT_DIMS = (((1,), (1,)), ((), ()))


def sigma_kernel(
    n_dev,
    group,
    x_ref,
    occ_ref,
    vir_ref,
    coul_hbm,
    oo_hbm,
    vv_hbm,
    sigma_ref,
    update_ref,
    coul,
    oo,
    vv,
    x_pad,
    gathered,
    x_t,
    total,
    outgoing,
    incoming,
    scalars_out,
    scalars_in,
    norms_out,
    norms_in,
    halfway_a,
    halfway_b,
    load_sem,
    gather_send,
    gather_recv,
    sum_send,
    sum_recv,
    scalar_send,
    scalar_recv,
    norm_send,
    norm_recv,
):
    me = lax.axis_index("aux")
    n_trial, rows, n_virt = x_ref.shape
    aux_local, n_occ, _ = oo.shape
    width = x_pad.shape[1]
    half_trials = n_trial // 2
    half_cols = half_trials * n_occ
    f32, bf16 = jnp.float32, jnp.bfloat16

    loads = [
        pltpu.make_async_copy(source, target, load_sem.at[slot])
        for slot, (source, target) in enumerate(((coul_hbm, coul), (vv_hbm, vv), (oo_hbm, oo)))
    ]
    for load in loads:
        load.start()

    barrier = pltpu.get_barrier_semaphore()

    def greet(step, carry):
        pl.semaphore_signal(
            barrier, inc=1, device_id={"aux": lax.rem(me + step, n_dev)}, device_id_type=MESH
        )
        return carry

    lax.fori_loop(1, n_dev, greet, 0)

    x_pad[...] = jnp.zeros_like(x_pad)
    x_pad[:, :n_virt] = x_ref[...].reshape(n_trial * rows, n_virt)
    gathered[me] = x_pad[...].astype(bf16)
    pl.semaphore_wait(barrier, n_dev - 1)

    def to_peer(source, target, send_sem, recv_sem, step):
        return pltpu.make_async_remote_copy(
            src_ref=source,
            dst_ref=target,
            send_sem=send_sem.at[step],
            recv_sem=recv_sem.at[step],
            device_id={"aux": lax.rem(me + step, n_dev)},
            device_id_type=MESH,
        )

    def gather_copy(step):
        return to_peer(gathered.at[me], gathered.at[me], gather_send, gather_recv, step)

    def sum_copy(half, step):
        peer = lax.rem(me + step, n_dev)
        return to_peer(
            outgoing.at[half, peer], incoming.at[half, me], sum_send.at[half], sum_recv.at[half], step
        )

    def scalar_copy(step):
        return to_peer(scalars_out, scalars_in.at[me], scalar_send, scalar_recv, step)

    def norm_copy(step):
        return to_peer(norms_out, norms_in.at[me], norm_send, norm_recv, step)

    def each(action):
        def body(step, carry):
            action(step)
            return carry

        lax.fori_loop(1, n_dev, body, 0)

    each(lambda step: gather_copy(step).start())
    for load in loads:
        load.wait()
    each(lambda step: gather_copy(step).wait_recv())

    wide = gathered[...].astype(f32).reshape(n_dev, n_trial, rows, width)
    for n in range(n_trial):
        x_t[:, n * n_occ : (n + 1) * n_occ] = (
            wide[:, n].reshape(n_occ, width).T.astype(bf16)
        )

    block = 16
    pairs = n_virt // (2 * block)
    z_rows, z_cols = n_trial * block, aux_local * block

    def coul_block(pair):
        return jnp.concatenate(
            [
                coul[:, (2 * pair + t) * block : (2 * pair + t + 1) * block, :].reshape(z_cols, n_occ)
                for t in range(2)
            ],
            axis=1,
        )

    z = jnp.zeros((z_rows, z_cols), f32)
    for pair in range(pairs):
        left = jnp.concatenate(
            [
                jnp.concatenate(
                    [
                        x_t[
                            (2 * pair + t) * block : (2 * pair + t + 1) * block,
                            n * n_occ : (n + 1) * n_occ,
                        ]
                        for n in range(n_trial)
                    ],
                    axis=0,
                )
                for t in range(2)
            ],
            axis=1,
        )
        z = z + lax.dot_general(left, coul_block(pair), NT_DIMS, preferred_element_type=f32)
    same = (
        lax.broadcasted_iota(jnp.int32, (z_rows, z_cols), 0) % block
        == lax.broadcasted_iota(jnp.int32, (z_rows, z_cols), 1) % block
    )
    z = jnp.sum(jnp.where(same, z, 0.0).reshape(n_trial, block, z_cols), axis=1)
    lanes = 128
    chunks = z_cols // lanes
    ones = (
        lax.broadcasted_iota(jnp.int32, (lanes, lanes), 0) // block
        == lax.broadcasted_iota(jnp.int32, (lanes, lanes), 1) // block
    ).astype(bf16)
    z = jnp.concatenate([z[:, c * lanes : (c + 1) * lanes] for c in range(chunks)], axis=0)
    coef = jnp.zeros_like(z)
    for _ in range(3):
        piece = z.astype(bf16)
        z = z - piece.astype(f32)
        coef = coef + jnp.dot(piece, ones, preferred_element_type=f32)
    coef = jnp.concatenate(
        [coef[c * n_trial : (c + 1) * n_trial] for c in range(chunks)], axis=1
    )
    coef = jnp.broadcast_to(coef[:, None, :], (n_trial, block, z_cols)).reshape(z_rows, z_cols)
    spread = jnp.where(same, coef, 0.0).astype(bf16)
    total[...] = jnp.zeros_like(total)
    for pair in range(pairs):
        part = 2.0 * jnp.dot(spread, coul_block(pair), preferred_element_type=f32)
        for t in range(2):
            for n in range(n_trial):
                total[n, (2 * pair + t) * block : (2 * pair + t + 1) * block, :] = part[
                    n * block : (n + 1) * block, t * n_occ : (t + 1) * n_occ
                ]

    for half in range(2):
        x_half = x_t[:n_virt, half * half_cols : (half + 1) * half_cols]

        def first_step(index, slot, x_half=x_half):
            slot[...] = jnp.dot(
                vv[pl.ds(index * group, group)].reshape(group * n_virt, n_virt),
                x_half,
                preferred_element_type=f32,
            ).astype(bf16)

        def second_step(index, slot, half=half):
            left = jnp.concatenate(
                [
                    jnp.concatenate(
                        [
                            slot[p * n_virt : (p + 1) * n_virt, n * n_occ : (n + 1) * n_occ]
                            for p in range(group)
                        ],
                        axis=1,
                    )
                    for n in range(half_trials)
                ],
                axis=0,
            )
            right = jnp.concatenate([oo[index * group + p] for p in range(group)], axis=1)
            part = lax.dot_general(left, right, NT_DIMS, preferred_element_type=f32)
            for n in range(half_trials):
                at = half * half_trials + n
                total[at, :n_virt, :] = (
                    total[at, :n_virt, :] - part[n * n_virt : (n + 1) * n_virt, :]
                )

        def exchange(index, carry):
            first_step(2 * index + 1, halfway_b)
            second_step(2 * index, halfway_a)
            first_step(2 * index + 2, halfway_a)
            second_step(2 * index + 1, halfway_b)
            return carry

        groups = aux_local // group
        first_step(0, halfway_a)
        lax.fori_loop(0, groups // 2 - 1, exchange, 0)
        first_step(groups - 1, halfway_b)
        second_step(groups - 2, halfway_a)
        second_step(groups - 1, halfway_b)
        outgoing[half] = jnp.concatenate(
            [
                total[half * half_trials + n].T.reshape(n_dev, rows, width)
                for n in range(half_trials)
            ],
            axis=1,
        ).astype(bf16)
        each(lambda step, half=half: sum_copy(half, step).start())
        incoming[half, me] = outgoing[half, me]

    row_at = lax.broadcasted_iota(jnp.int32, (rows, n_occ), 0) + me * rows
    col_at = lax.broadcasted_iota(jnp.int32, (rows, n_occ), 1)
    occ_rows = jnp.sum(jnp.where(row_at == col_at, occ_ref[...], 0.0), axis=1, keepdims=True)
    diagonal = vir_ref[...] - occ_rows

    def whole(value):
        return jnp.sum(jnp.sum(value, axis=0, keepdims=True), axis=1, keepdims=True)

    numer, denom = [], []
    for n in range(n_trial):
        own = x_ref[n]
        square = own * own
        x_n = x_t[:, n * n_occ : (n + 1) * n_occ].astype(f32)
        numer.append(whole(x_n * total[n]) + whole(diagonal * square))
        denom.append(whole(square))
    for n in range(n_trial):
        scalars_out[n : n + 1, :] = jnp.broadcast_to(numer[n], (1, lanes))
        scalars_out[n_trial + n : n_trial + n + 1, :] = jnp.broadcast_to(denom[n], (1, lanes))
    each(lambda step: scalar_copy(step).start())
    scalars_in[me] = scalars_out[...]

    for half in range(2):
        each(lambda step, half=half: sum_copy(half, step).wait_recv())
    each(lambda step: scalar_copy(step).wait_recv())

    sums = jnp.sum(scalars_in[...], axis=0)
    precond = []
    for n in range(n_trial):
        if n % half_trials == 0:
            summed = jnp.sum(incoming[n // half_trials].astype(f32), axis=0)
        at = (n % half_trials) * rows
        own = x_ref[n]
        sigma = diagonal * own + summed[at : at + rows, :n_virt]
        sigma_ref[n] = sigma
        omega = sums[n : n + 1, :1] / (sums[n_trial + n : n_trial + n + 1, :1] + 1e-06)
        resid = sigma - omega * own
        precond.append(resid / jnp.maximum(jnp.abs(diagonal - omega), 1.0))
        norms_out[n : n + 1, :] = jnp.broadcast_to(whole(precond[n] * precond[n]), (1, lanes))
    each(lambda step: norm_copy(step).start())
    norms_in[me] = norms_out[...]
    each(lambda step: norm_copy(step).wait_recv())
    norms = jnp.sum(norms_in[...], axis=0)
    count = float(n_occ * n_virt)
    for n in range(n_trial):
        update_ref[n] = precond[n] * lax.rsqrt(norms[n : n + 1, :1] / count + 1e-06)

    each(lambda step: gather_copy(step).wait_send())
    for half in range(2):
        each(lambda step, half=half: sum_copy(half, step).wait_send())
    each(lambda step: scalar_copy(step).wait_send())
    each(lambda step: norm_copy(step).wait_send())


def on_device(n_dev, trial_vecs, occ_energy, vir_energy, coul_ov, exch_oo, exch_vv):
    n_trial, rows, n_virt = trial_vecs.shape
    aux_local, n_occ, _ = exch_oo.shape
    width = -(-n_virt // 128) * 128
    half_rows = n_trial // 2 * rows
    group = math.gcd(aux_local // 2, 8)
    vmem = pl.BlockSpec(memory_space=pltpu.VMEM)
    anywhere = pl.BlockSpec(memory_space=pl.ANY)
    out = jax.ShapeDtypeStruct(trial_vecs.shape, jnp.float32)
    dma = pltpu.SemaphoreType.DMA
    return pl.pallas_call(
        functools.partial(sigma_kernel, n_dev, group),
        out_shape=(out, out),
        in_specs=[vmem] * 3 + [anywhere] * 3,
        out_specs=(vmem, vmem),
        scratch_shapes=[
            pltpu.VMEM((aux_local, n_virt, n_occ), jnp.bfloat16),
            pltpu.VMEM((aux_local, n_occ, n_occ), jnp.bfloat16),
            pltpu.VMEM((aux_local, n_virt, n_virt), jnp.bfloat16),
            pltpu.VMEM((n_trial * rows, width), jnp.float32),
            pltpu.VMEM((n_dev, n_trial * rows, width), jnp.bfloat16),
            pltpu.VMEM((width, n_trial * n_occ), jnp.bfloat16),
            pltpu.VMEM((n_trial, width, n_occ), jnp.float32),
            pltpu.VMEM((2, n_dev, half_rows, width), jnp.bfloat16),
            pltpu.VMEM((2, n_dev, half_rows, width), jnp.bfloat16),
            pltpu.VMEM((2 * n_trial, 128), jnp.float32),
            pltpu.VMEM((n_dev, 2 * n_trial, 128), jnp.float32),
            pltpu.VMEM((2 * n_trial, 128), jnp.float32),
            pltpu.VMEM((n_dev, 2 * n_trial, 128), jnp.float32),
            pltpu.VMEM((group * n_virt, n_trial // 2 * n_occ), jnp.bfloat16),
            pltpu.VMEM((group * n_virt, n_trial // 2 * n_occ), jnp.bfloat16),
            dma((3,)),
            dma((n_dev,)),
            dma((n_dev,)),
            dma((2, n_dev)),
            dma((2, n_dev)),
            dma((n_dev,)),
            dma((n_dev,)),
            dma((n_dev,)),
            dma((n_dev,)),
        ],
        compiler_params=pltpu.CompilerParams(
            collective_id=0, has_side_effects=True, vmem_limit_bytes=56 * 1024 * 1024
        ),
    )(
        trial_vecs,
        occ_energy[None, :],
        vir_energy[None, :],
        coul_ov.transpose(0, 2, 1),
        exch_oo,
        exch_vv,
    )


def contract(rows_x, coul_ov, exch_oo, exch_vv):
    aux_coef = jnp.einsum("pia,nia->np", coul_ov, rows_x, preferred_element_type=jnp.float32)
    coulomb = jnp.einsum(
        "pia,np->nia", coul_ov, aux_coef.astype(jnp.bfloat16), preferred_element_type=jnp.float32
    )
    aux_local, n_occ, _ = exch_oo.shape
    n_virt = exch_vv.shape[1]
    group_size = math.gcd(aux_local, 16)
    vv_groups = exch_vv.reshape(aux_local // group_size, group_size, n_virt, n_virt)
    oo_groups = exch_oo.reshape(aux_local // group_size, group_size, n_occ, n_occ)

    def advance(running, parts_pair):
        vv_part, oo_part = parts_pair
        halfway = jnp.einsum(
            "pab,njb->pnja", vv_part, rows_x, preferred_element_type=jnp.float32
        ).astype(jnp.bfloat16)
        return (
            running
            + jnp.einsum("pij,pnja->nia", oo_part, halfway, preferred_element_type=jnp.float32),
            None,
        )

    exchange, _ = lax.scan(advance, jnp.zeros(rows_x.shape, jnp.float32), (vv_groups, oo_groups))
    return 2.0 * coulomb - exchange


def on_device_plain(trial_vecs, occ_energy, vir_energy, coul_ov, exch_oo, exch_vv):
    local_rows = trial_vecs.shape[1]
    n_occ, n_virt = coul_ov.shape[1:]
    row_start = lax.axis_index("aux") * local_rows
    rows_x = lax.all_gather(trial_vecs.astype(jnp.bfloat16), "aux", axis=1, tiled=True)
    summed = lax.psum_scatter(
        contract(rows_x, coul_ov, exch_oo, exch_vv), "aux", scatter_dimension=1, tiled=True
    )
    occ_rows = lax.dynamic_slice_in_dim(occ_energy, row_start, local_rows, 0)
    diagonal = vir_energy[None, :] - occ_rows[:, None]
    sigma = diagonal[None] * trial_vecs + summed
    sums = lax.psum(
        jnp.stack([jnp.sum(trial_vecs * sigma, (1, 2)), jnp.sum(trial_vecs * trial_vecs, (1, 2))]),
        "aux",
    )
    omega = (sums[0] / (sums[1] + 1e-06))[:, None, None]
    precond = (sigma - omega * trial_vecs) / jnp.maximum(jnp.abs(diagonal[None] - omega), 1.0)
    squares = lax.psum(jnp.sum(precond * precond, axis=(1, 2)), "aux") / (n_occ * n_virt)
    return sigma, precond * lax.rsqrt(squares + 1e-06)[:, None, None]


def solution(mesh):
    n_dev = mesh.shape["aux"]

    def body(trial_vecs, occ_energy, vir_energy, coul_ov, exch_oo, exch_vv):
        n_trial, rows, n_virt = trial_vecs.shape
        aux_local, n_occ, _ = exch_oo.shape
        tiled = (
            n_trial % 4 == 0
            and rows % 8 == 0
            and n_occ % 128 == 0
            and n_virt % 32 == 0
            and aux_local % 16 == 0
        )
        args = (trial_vecs, occ_energy, vir_energy, coul_ov, exch_oo, exch_vv)
        return on_device(n_dev, *args) if tiled else on_device_plain(*args)

    in_specs = (
        P("geom", "aux", None),
        P("geom"),
        P("geom"),
        P(("geom", "aux"), None, None),
        P(("geom", "aux"), None, None),
        P(("geom", "aux"), None, None),
    )
    out_specs = (P("geom", "aux", None), P("geom", "aux", None))
    return jax.shard_map(body, mesh=mesh, in_specs=in_specs, out_specs=out_specs, check_vma=False)
```

```python
import functools
import math

import jax
import jax.numpy as jnp
from jax import lax
from jax.experimental import pallas as pl
from jax.experimental.pallas import tpu as pltpu
from jax.sharding import PartitionSpec as P

MESH = pl.DeviceIdType.MESH
NT_DIMS = (((1,), (1,)), ((), ()))


def sigma_kernel(
    n_dev,
    group,
    x_ref,
    occ_ref,
    vir_ref,
    coul_hbm,
    oo_hbm,
    vv_hbm,
    sigma_ref,
    update_ref,
    coul,
    oo,
    vv,
    x_pad,
    gathered,
    x_t,
    total,
    outgoing,
    incoming,
    scalars_out,
    scalars_in,
    norms_out,
    norms_in,
    halfway_a,
    halfway_b,
    load_sem,
    gather_send,
    gather_recv,
    sum_send,
    sum_recv,
    scalar_send,
    scalar_recv,
    norm_send,
    norm_recv,
):
    me = lax.axis_index("aux")
    n_trial, rows, n_virt = x_ref.shape
    aux_local, n_occ, _ = oo.shape
    width = x_pad.shape[1]
    half_trials = n_trial // 2
    half_cols = half_trials * n_occ
    f32, bf16 = jnp.float32, jnp.bfloat16

    loads = [
        pltpu.make_async_copy(source, target, load_sem.at[slot])
        for slot, (source, target) in enumerate(((coul_hbm, coul), (vv_hbm, vv), (oo_hbm, oo)))
    ]
    for load in loads:
        load.start()

    barrier = pltpu.get_barrier_semaphore()

    def greet(step, carry):
        pl.semaphore_signal(
            barrier, inc=1, device_id={"aux": lax.rem(me + step, n_dev)}, device_id_type=MESH
        )
        return carry

    lax.fori_loop(1, n_dev, greet, 0)

    x_pad[...] = jnp.zeros_like(x_pad)
    x_pad[:, :n_virt] = x_ref[...].reshape(n_trial * rows, n_virt)
    gathered[me] = x_pad[...].astype(bf16)
    pl.semaphore_wait(barrier, n_dev - 1)

    def to_peer(source, target, send_sem, recv_sem, step):
        return pltpu.make_async_remote_copy(
            src_ref=source,
            dst_ref=target,
            send_sem=send_sem.at[step],
            recv_sem=recv_sem.at[step],
            device_id={"aux": lax.rem(me + step, n_dev)},
            device_id_type=MESH,
        )

    pair = me + 1 - 2 * lax.rem(me, 2)
    chip_steps = sorted(range(2, n_dev, 2), key=lambda step: -min(step, n_dev - step))

    def block_copy(owner, peer, sem_at):
        return pltpu.make_async_remote_copy(
            src_ref=gathered.at[owner],
            dst_ref=gathered.at[owner],
            send_sem=gather_send.at[sem_at],
            recv_sem=gather_recv.at[sem_at],
            device_id={"aux": peer},
            device_id_type=MESH,
        )

    def direct_copy(step):
        return block_copy(me, lax.rem(me + step, n_dev), step)

    def passed_copy(step):
        return block_copy(lax.rem(me + n_dev - step, n_dev), pair, step + 1)

    def sum_copy(half, step):
        peer = lax.rem(me + step, n_dev)
        return to_peer(
            outgoing.at[half, peer], incoming.at[half, me], sum_send.at[half], sum_recv.at[half], step
        )

    def scalar_copy(step):
        return to_peer(scalars_out, scalars_in.at[me], scalar_send, scalar_recv, step)

    def norm_copy(step):
        return to_peer(norms_out, norms_in.at[me], norm_send, norm_recv, step)

    def each(action):
        def body(step, carry):
            action(step)
            return carry

        lax.fori_loop(1, n_dev, body, 0)

    for step in chip_steps:
        direct_copy(step).start()
    block_copy(me, pair, 1).start()
    for load in loads:
        load.wait()
    for step in reversed(chip_steps):
        direct_copy(step).wait_recv()
        passed_copy(step).start()
    block_copy(me, pair, 1).wait_recv()
    for step in reversed(chip_steps):
        passed_copy(step).wait_recv()

    wide = gathered[...].astype(f32).reshape(n_dev, n_trial, rows, width)
    for n in range(n_trial):
        x_t[:, n * n_occ : (n + 1) * n_occ] = (
            wide[:, n].reshape(n_occ, width).T.astype(bf16)
        )

    block = 16
    pairs = n_virt // (2 * block)
    z_rows, z_cols = n_trial * block, aux_local * block

    def coul_block(pair):
        return jnp.concatenate(
            [
                coul[:, (2 * pair + t) * block : (2 * pair + t + 1) * block, :].reshape(z_cols, n_occ)
                for t in range(2)
            ],
            axis=1,
        )

    z = jnp.zeros((z_rows, z_cols), f32)
    for pair in range(pairs):
        left = jnp.concatenate(
            [
                jnp.concatenate(
                    [
                        x_t[
                            (2 * pair + t) * block : (2 * pair + t + 1) * block,
                            n * n_occ : (n + 1) * n_occ,
                        ]
                        for n in range(n_trial)
                    ],
                    axis=0,
                )
                for t in range(2)
            ],
            axis=1,
        )
        z = z + lax.dot_general(left, coul_block(pair), NT_DIMS, preferred_element_type=f32)
    same = (
        lax.broadcasted_iota(jnp.int32, (z_rows, z_cols), 0) % block
        == lax.broadcasted_iota(jnp.int32, (z_rows, z_cols), 1) % block
    )
    z = jnp.sum(jnp.where(same, z, 0.0).reshape(n_trial, block, z_cols), axis=1)
    lanes = 128
    chunks = z_cols // lanes
    ones = (
        lax.broadcasted_iota(jnp.int32, (lanes, lanes), 0) // block
        == lax.broadcasted_iota(jnp.int32, (lanes, lanes), 1) // block
    ).astype(bf16)
    z = jnp.concatenate([z[:, c * lanes : (c + 1) * lanes] for c in range(chunks)], axis=0)
    coef = jnp.zeros_like(z)
    for _ in range(3):
        piece = z.astype(bf16)
        z = z - piece.astype(f32)
        coef = coef + jnp.dot(piece, ones, preferred_element_type=f32)
    coef = jnp.concatenate(
        [coef[c * n_trial : (c + 1) * n_trial] for c in range(chunks)], axis=1
    )
    coef = jnp.broadcast_to(coef[:, None, :], (n_trial, block, z_cols)).reshape(z_rows, z_cols)
    spread = jnp.where(same, coef, 0.0).astype(bf16)
    total[...] = jnp.zeros_like(total)
    for pair in range(pairs):
        part = 2.0 * jnp.dot(spread, coul_block(pair), preferred_element_type=f32)
        for t in range(2):
            for n in range(n_trial):
                total[n, (2 * pair + t) * block : (2 * pair + t + 1) * block, :] = part[
                    n * block : (n + 1) * block, t * n_occ : (t + 1) * n_occ
                ]

    for half in range(2):
        x_half = x_t[:n_virt, half * half_cols : (half + 1) * half_cols]

        def first_step(index, slot, x_half=x_half):
            slot[...] = jnp.dot(
                vv[pl.ds(index * group, group)].reshape(group * n_virt, n_virt),
                x_half,
                preferred_element_type=f32,
            ).astype(bf16)

        def second_step(index, slot, half=half):
            left = jnp.concatenate(
                [
                    jnp.concatenate(
                        [
                            slot[p * n_virt : (p + 1) * n_virt, n * n_occ : (n + 1) * n_occ]
                            for p in range(group)
                        ],
                        axis=1,
                    )
                    for n in range(half_trials)
                ],
                axis=0,
            )
            right = jnp.concatenate([oo[index * group + p] for p in range(group)], axis=1)
            part = lax.dot_general(left, right, NT_DIMS, preferred_element_type=f32)
            for n in range(half_trials):
                at = half * half_trials + n
                total[at, :n_virt, :] = (
                    total[at, :n_virt, :] - part[n * n_virt : (n + 1) * n_virt, :]
                )

        def exchange(index, carry):
            first_step(2 * index + 1, halfway_b)
            second_step(2 * index, halfway_a)
            first_step(2 * index + 2, halfway_a)
            second_step(2 * index + 1, halfway_b)
            return carry

        groups = aux_local // group
        first_step(0, halfway_a)
        lax.fori_loop(0, groups // 2 - 1, exchange, 0)
        first_step(groups - 1, halfway_b)
        second_step(groups - 2, halfway_a)
        second_step(groups - 1, halfway_b)
        outgoing[half] = jnp.concatenate(
            [
                total[half * half_trials + n].T.reshape(n_dev, rows, width)
                for n in range(half_trials)
            ],
            axis=1,
        ).astype(bf16)
        each(lambda step, half=half: sum_copy(half, step).start())
        incoming[half, me] = outgoing[half, me]

    row_at = lax.broadcasted_iota(jnp.int32, (rows, n_occ), 0) + me * rows
    col_at = lax.broadcasted_iota(jnp.int32, (rows, n_occ), 1)
    occ_rows = jnp.sum(jnp.where(row_at == col_at, occ_ref[...], 0.0), axis=1, keepdims=True)
    diagonal = vir_ref[...] - occ_rows

    def whole(value):
        return jnp.sum(jnp.sum(value, axis=0, keepdims=True), axis=1, keepdims=True)

    numer, denom = [], []
    for n in range(n_trial):
        own = x_ref[n]
        square = own * own
        x_n = x_t[:, n * n_occ : (n + 1) * n_occ].astype(f32)
        numer.append(whole(x_n * total[n]) + whole(diagonal * square))
        denom.append(whole(square))
    for n in range(n_trial):
        scalars_out[n : n + 1, :] = jnp.broadcast_to(numer[n], (1, lanes))
        scalars_out[n_trial + n : n_trial + n + 1, :] = jnp.broadcast_to(denom[n], (1, lanes))
    each(lambda step: scalar_copy(step).start())
    scalars_in[me] = scalars_out[...]

    for half in range(2):
        each(lambda step, half=half: sum_copy(half, step).wait_recv())
    each(lambda step: scalar_copy(step).wait_recv())

    sums = jnp.sum(scalars_in[...], axis=0)
    precond = []
    for n in range(n_trial):
        if n % half_trials == 0:
            summed = jnp.sum(incoming[n // half_trials].astype(f32), axis=0)
        at = (n % half_trials) * rows
        own = x_ref[n]
        sigma = diagonal * own + summed[at : at + rows, :n_virt]
        sigma_ref[n] = sigma
        omega = sums[n : n + 1, :1] / (sums[n_trial + n : n_trial + n + 1, :1] + 1e-06)
        resid = sigma - omega * own
        precond.append(resid / jnp.maximum(jnp.abs(diagonal - omega), 1.0))
        norms_out[n : n + 1, :] = jnp.broadcast_to(whole(precond[n] * precond[n]), (1, lanes))
    each(lambda step: norm_copy(step).start())
    norms_in[me] = norms_out[...]
    each(lambda step: norm_copy(step).wait_recv())
    norms = jnp.sum(norms_in[...], axis=0)
    count = float(n_occ * n_virt)
    for n in range(n_trial):
        update_ref[n] = precond[n] * lax.rsqrt(norms[n : n + 1, :1] / count + 1e-06)

    block_copy(me, pair, 1).wait_send()
    for step in chip_steps:
        direct_copy(step).wait_send()
        passed_copy(step).wait_send()
    for half in range(2):
        each(lambda step, half=half: sum_copy(half, step).wait_send())
    each(lambda step: scalar_copy(step).wait_send())
    each(lambda step: norm_copy(step).wait_send())


def hand_over(sigma_in, update_in, sigma_ref, update_ref):
    sigma_ref[...] = sigma_in[...]
    update_ref[...] = update_in[...]


def on_device(n_dev, trial_vecs, occ_energy, vir_energy, coul_ov, exch_oo, exch_vv):
    n_trial, rows, n_virt = trial_vecs.shape
    aux_local, n_occ, _ = exch_oo.shape
    width = -(-n_virt // 128) * 128
    half_rows = n_trial // 2 * rows
    group = math.gcd(aux_local // 2, 8)
    vmem = pl.BlockSpec(memory_space=pltpu.VMEM)
    anywhere = pl.BlockSpec(memory_space=pl.ANY)
    out = jax.ShapeDtypeStruct(trial_vecs.shape, jnp.float32)
    dma = pltpu.SemaphoreType.DMA
    sigma, update = pl.pallas_call(
        functools.partial(sigma_kernel, n_dev, group),
        out_shape=(out, out),
        in_specs=[vmem] * 3 + [anywhere] * 3,
        out_specs=(vmem, vmem),
        scratch_shapes=[
            pltpu.VMEM((aux_local, n_virt, n_occ), jnp.bfloat16),
            pltpu.VMEM((aux_local, n_occ, n_occ), jnp.bfloat16),
            pltpu.VMEM((aux_local, n_virt, n_virt), jnp.bfloat16),
            pltpu.VMEM((n_trial * rows, width), jnp.float32),
            pltpu.VMEM((n_dev, n_trial * rows, width), jnp.bfloat16),
            pltpu.VMEM((width, n_trial * n_occ), jnp.bfloat16),
            pltpu.VMEM((n_trial, width, n_occ), jnp.float32),
            pltpu.VMEM((2, n_dev, half_rows, width), jnp.bfloat16),
            pltpu.VMEM((2, n_dev, half_rows, width), jnp.bfloat16),
            pltpu.VMEM((2 * n_trial, 128), jnp.float32),
            pltpu.VMEM((n_dev, 2 * n_trial, 128), jnp.float32),
            pltpu.VMEM((2 * n_trial, 128), jnp.float32),
            pltpu.VMEM((n_dev, 2 * n_trial, 128), jnp.float32),
            pltpu.VMEM((group * n_virt, n_trial // 2 * n_occ), jnp.bfloat16),
            pltpu.VMEM((group * n_virt, n_trial // 2 * n_occ), jnp.bfloat16),
            dma((3,)),
            dma((n_dev,)),
            dma((n_dev,)),
            dma((2, n_dev)),
            dma((2, n_dev)),
            dma((n_dev,)),
            dma((n_dev,)),
            dma((n_dev,)),
            dma((n_dev,)),
        ],
        compiler_params=pltpu.CompilerParams(
            collective_id=0, has_side_effects=True, vmem_limit_bytes=56 * 1024 * 1024
        ),
    )(
        trial_vecs,
        occ_energy[None, :],
        vir_energy[None, :],
        coul_ov.transpose(0, 2, 1),
        exch_oo,
        exch_vv,
    )
    return pl.pallas_call(
        hand_over, out_shape=(out, out), in_specs=[vmem] * 2, out_specs=(vmem, vmem)
    )(sigma, update)


def contract(rows_x, coul_ov, exch_oo, exch_vv):
    aux_coef = jnp.einsum("pia,nia->np", coul_ov, rows_x, preferred_element_type=jnp.float32)
    coulomb = jnp.einsum(
        "pia,np->nia", coul_ov, aux_coef.astype(jnp.bfloat16), preferred_element_type=jnp.float32
    )
    aux_local, n_occ, _ = exch_oo.shape
    n_virt = exch_vv.shape[1]
    group_size = math.gcd(aux_local, 16)
    vv_groups = exch_vv.reshape(aux_local // group_size, group_size, n_virt, n_virt)
    oo_groups = exch_oo.reshape(aux_local // group_size, group_size, n_occ, n_occ)

    def advance(running, parts_pair):
        vv_part, oo_part = parts_pair
        halfway = jnp.einsum(
            "pab,njb->pnja", vv_part, rows_x, preferred_element_type=jnp.float32
        ).astype(jnp.bfloat16)
        return (
            running
            + jnp.einsum("pij,pnja->nia", oo_part, halfway, preferred_element_type=jnp.float32),
            None,
        )

    exchange, _ = lax.scan(advance, jnp.zeros(rows_x.shape, jnp.float32), (vv_groups, oo_groups))
    return 2.0 * coulomb - exchange


def on_device_plain(trial_vecs, occ_energy, vir_energy, coul_ov, exch_oo, exch_vv):
    local_rows = trial_vecs.shape[1]
    n_occ, n_virt = coul_ov.shape[1:]
    row_start = lax.axis_index("aux") * local_rows
    rows_x = lax.all_gather(trial_vecs.astype(jnp.bfloat16), "aux", axis=1, tiled=True)
    summed = lax.psum_scatter(
        contract(rows_x, coul_ov, exch_oo, exch_vv), "aux", scatter_dimension=1, tiled=True
    )
    occ_rows = lax.dynamic_slice_in_dim(occ_energy, row_start, local_rows, 0)
    diagonal = vir_energy[None, :] - occ_rows[:, None]
    sigma = diagonal[None] * trial_vecs + summed
    sums = lax.psum(
        jnp.stack([jnp.sum(trial_vecs * sigma, (1, 2)), jnp.sum(trial_vecs * trial_vecs, (1, 2))]),
        "aux",
    )
    omega = (sums[0] / (sums[1] + 1e-06))[:, None, None]
    precond = (sigma - omega * trial_vecs) / jnp.maximum(jnp.abs(diagonal[None] - omega), 1.0)
    squares = lax.psum(jnp.sum(precond * precond, axis=(1, 2)), "aux") / (n_occ * n_virt)
    return sigma, precond * lax.rsqrt(squares + 1e-06)[:, None, None]


def solution(mesh):
    n_dev = mesh.shape["aux"]

    def body(trial_vecs, occ_energy, vir_energy, coul_ov, exch_oo, exch_vv):
        n_trial, rows, n_virt = trial_vecs.shape
        aux_local, n_occ, _ = exch_oo.shape
        tiled = (
            n_trial % 4 == 0
            and rows % 8 == 0
            and n_occ % 128 == 0
            and n_virt % 32 == 0
            and aux_local % 16 == 0
            and n_dev % 2 == 0
        )
        args = (trial_vecs, occ_energy, vir_energy, coul_ov, exch_oo, exch_vv)
        return on_device(n_dev, *args) if tiled else on_device_plain(*args)

    in_specs = (
        P("geom", "aux", None),
        P("geom"),
        P("geom"),
        P(("geom", "aux"), None, None),
        P(("geom", "aux"), None, None),
        P(("geom", "aux"), None, None),
    )
    out_specs = (P("geom", "aux", None), P("geom", "aux", None))
    return jax.shard_map(body, mesh=mesh, in_specs=in_specs, out_specs=out_specs, check_vma=False)
```

```python
import functools
import math

import jax
import jax.numpy as jnp
from jax import lax
from jax.experimental import pallas as pl
from jax.experimental.pallas import tpu as pltpu
from jax.sharding import PartitionSpec as P

MESH = pl.DeviceIdType.MESH


def sigma_kernel(
    n_dev,
    group,
    x_ref,
    occ_ref,
    vir_ref,
    coul_hbm,
    oo_hbm,
    vv_hbm,
    sigma_ref,
    update_ref,
    coul,
    oo,
    vv,
    x_pad,
    gathered,
    x_t,
    total,
    outgoing,
    incoming,
    scalars_out,
    scalars_in,
    norms_out,
    norms_in,
    halfway_a,
    halfway_b,
    coul_t,
    oo_t,
    load_sem,
    gather_send,
    gather_recv,
    sum_send,
    sum_recv,
    scalar_send,
    scalar_recv,
    norm_send,
    norm_recv,
):
    me = lax.axis_index("aux")
    n_trial, rows, n_virt = x_ref.shape
    aux_local, n_occ, _ = oo.shape
    width = x_pad.shape[1]
    half_trials = n_trial // 2
    half_cols = half_trials * n_occ
    f32, bf16 = jnp.float32, jnp.bfloat16

    loads = [
        pltpu.make_async_copy(source, target, load_sem.at[slot])
        for slot, (source, target) in enumerate(((coul_hbm, coul), (oo_hbm, oo), (vv_hbm, vv)))
    ]
    for load in loads:
        load.start()

    barrier = pltpu.get_barrier_semaphore()

    def greet(step, carry):
        pl.semaphore_signal(
            barrier, inc=1, device_id={"aux": lax.rem(me + step, n_dev)}, device_id_type=MESH
        )
        return carry

    lax.fori_loop(1, n_dev, greet, 0)

    x_pad[...] = jnp.zeros_like(x_pad)
    x_pad[:, :n_virt] = x_ref[...].reshape(n_trial * rows, n_virt)
    gathered[me] = x_pad[...].astype(bf16)
    pl.semaphore_wait(barrier, n_dev - 1)

    def to_peer(source, target, send_sem, recv_sem, step):
        return pltpu.make_async_remote_copy(
            src_ref=source,
            dst_ref=target,
            send_sem=send_sem.at[step],
            recv_sem=recv_sem.at[step],
            device_id={"aux": lax.rem(me + step, n_dev)},
            device_id_type=MESH,
        )

    pair = me + 1 - 2 * lax.rem(me, 2)
    chip_steps = sorted(range(2, n_dev, 2), key=lambda step: -min(step, n_dev - step))

    def block_copy(owner, peer, sem_at):
        return pltpu.make_async_remote_copy(
            src_ref=gathered.at[owner],
            dst_ref=gathered.at[owner],
            send_sem=gather_send.at[sem_at],
            recv_sem=gather_recv.at[sem_at],
            device_id={"aux": peer},
            device_id_type=MESH,
        )

    def direct_copy(step):
        return block_copy(me, lax.rem(me + step, n_dev), step)

    def passed_copy(step):
        return block_copy(lax.rem(me + n_dev - step, n_dev), pair, step + 1)

    def sum_copy(half, step):
        peer = lax.rem(me + step, n_dev)
        return to_peer(
            outgoing.at[half, peer], incoming.at[half, me], sum_send.at[half], sum_recv.at[half], step
        )

    def scalar_copy(step):
        return to_peer(scalars_out, scalars_in.at[me], scalar_send, scalar_recv, step)

    def norm_copy(step):
        return to_peer(norms_out, norms_in.at[me], norm_send, norm_recv, step)

    def each(action):
        def body(step, carry):
            action(step)
            return carry

        lax.fori_loop(1, n_dev, body, 0)

    for step in chip_steps:
        direct_copy(step).start()
    block_copy(me, pair, 1).start()

    block = 16
    tiles = n_virt // block
    z_rows, z_cols = n_trial * block, aux_local * block
    loads[0].wait()
    for t in range(tiles):
        coul_t[t * n_occ : (t + 1) * n_occ, :] = (
            coul[:, t * block : (t + 1) * block, :].reshape(z_cols, n_occ).T
        )
    loads[1].wait()

    def turn(index, carry):
        for p in range(group):
            at = index * group + p
            oo_t[pl.ds(at * n_occ, n_occ), :] = oo[at].T
        return carry

    lax.fori_loop(0, aux_local // group, turn, 0)
    loads[2].wait()
    for step in reversed(chip_steps):
        direct_copy(step).wait_recv()
        passed_copy(step).start()
    block_copy(me, pair, 1).wait_recv()
    for step in reversed(chip_steps):
        passed_copy(step).wait_recv()

    wide = gathered[...].astype(f32).reshape(n_dev, n_trial, rows, width)
    for n in range(n_trial):
        x_t[:, n * n_occ : (n + 1) * n_occ] = (
            wide[:, n].reshape(n_occ, width).T.astype(bf16)
        )

    def first_step(half, index, slot):
        slot[...] = jnp.dot(
            vv[pl.ds(index * group, group)].reshape(group * n_virt, n_virt),
            x_t[:n_virt, half * half_cols : (half + 1) * half_cols],
            preferred_element_type=f32,
        ).astype(bf16)

    first_step(0, 0, halfway_a)

    left = jnp.concatenate(
        [
            jnp.concatenate(
                [
                    x_t[t * block : (t + 1) * block, n * n_occ : (n + 1) * n_occ]
                    for n in range(n_trial)
                ],
                axis=0,
            )
            for t in range(tiles)
        ],
        axis=1,
    )
    z = jnp.dot(left, coul_t[...], preferred_element_type=f32)
    same = (
        lax.broadcasted_iota(jnp.int32, (z_rows, z_cols), 0) % block
        == lax.broadcasted_iota(jnp.int32, (z_rows, z_cols), 1) % block
    )
    z = jnp.sum(jnp.where(same, z, 0.0).reshape(n_trial, block, z_cols), axis=1)
    lanes = 128
    chunks = z_cols // lanes
    ones = (
        lax.broadcasted_iota(jnp.int32, (lanes, lanes), 0) // block
        == lax.broadcasted_iota(jnp.int32, (lanes, lanes), 1) // block
    ).astype(bf16)
    z = jnp.concatenate([z[:, c * lanes : (c + 1) * lanes] for c in range(chunks)], axis=0)
    coef = jnp.zeros_like(z)
    for _ in range(3):
        piece = z.astype(bf16)
        z = z - piece.astype(f32)
        coef = coef + jnp.dot(piece, ones, preferred_element_type=f32)
    coef = jnp.concatenate(
        [coef[c * n_trial : (c + 1) * n_trial] for c in range(chunks)], axis=1
    )
    coef = jnp.broadcast_to(coef[:, None, :], (n_trial, block, z_cols)).reshape(z_rows, z_cols)
    spread = jnp.where(same, coef, 0.0).astype(bf16)
    total[...] = jnp.zeros_like(total)
    for pair in range(tiles // 2):
        right = jnp.concatenate(
            [
                coul[:, (2 * pair + t) * block : (2 * pair + t + 1) * block, :].reshape(z_cols, n_occ)
                for t in range(2)
            ],
            axis=1,
        )
        part = 2.0 * jnp.dot(spread, right, preferred_element_type=f32)
        for t in range(2):
            for n in range(n_trial):
                total[n, (2 * pair + t) * block : (2 * pair + t + 1) * block, :] = part[
                    n * block : (n + 1) * block, t * n_occ : (t + 1) * n_occ
                ]

    for half in range(2):
        def second_step(index, slot, half=half):
            left = jnp.concatenate(
                [
                    jnp.concatenate(
                        [
                            slot[p * n_virt : (p + 1) * n_virt, n * n_occ : (n + 1) * n_occ]
                            for p in range(group)
                        ],
                        axis=1,
                    )
                    for n in range(half_trials)
                ],
                axis=0,
            )
            right = oo_t[pl.ds(index * (group * n_occ), group * n_occ), :]
            part = jnp.dot(left, right, preferred_element_type=f32)
            for n in range(half_trials):
                at = half * half_trials + n
                total[at, :n_virt, :] = (
                    total[at, :n_virt, :] - part[n * n_virt : (n + 1) * n_virt, :]
                )

        def exchange(index, carry, half=half):
            first_step(half, 2 * index + 1, halfway_b)
            second_step(2 * index, halfway_a)
            first_step(half, 2 * index + 2, halfway_a)
            second_step(2 * index + 1, halfway_b)
            return carry

        groups = aux_local // group
        lax.fori_loop(0, groups // 2 - 1, exchange, 0)
        first_step(half, groups - 1, halfway_b)
        second_step(groups - 2, halfway_a)
        if half == 0:
            first_step(1, 0, halfway_a)
        second_step(groups - 1, halfway_b)
        outgoing[half] = jnp.concatenate(
            [
                total[half * half_trials + n].T.reshape(n_dev, rows, width)
                for n in range(half_trials)
            ],
            axis=1,
        ).astype(bf16)
        each(lambda step, half=half: sum_copy(half, step).start())
        incoming[half, me] = outgoing[half, me]

    row_at = lax.broadcasted_iota(jnp.int32, (rows, n_occ), 0) + me * rows
    col_at = lax.broadcasted_iota(jnp.int32, (rows, n_occ), 1)
    occ_rows = jnp.sum(jnp.where(row_at == col_at, occ_ref[...], 0.0), axis=1, keepdims=True)
    diagonal = vir_ref[...] - occ_rows

    def whole(value):
        return jnp.sum(jnp.sum(value, axis=0, keepdims=True), axis=1, keepdims=True)

    numer, denom = [], []
    for n in range(n_trial):
        own = x_ref[n]
        square = own * own
        x_n = x_t[:, n * n_occ : (n + 1) * n_occ].astype(f32)
        numer.append(whole(x_n * total[n]) + whole(diagonal * square))
        denom.append(whole(square))
    for n in range(n_trial):
        scalars_out[n : n + 1, :] = jnp.broadcast_to(numer[n], (1, lanes))
        scalars_out[n_trial + n : n_trial + n + 1, :] = jnp.broadcast_to(denom[n], (1, lanes))
    each(lambda step: scalar_copy(step).start())
    scalars_in[me] = scalars_out[...]

    for half in range(2):
        each(lambda step, half=half: sum_copy(half, step).wait_recv())
    each(lambda step: scalar_copy(step).wait_recv())

    sums = jnp.sum(scalars_in[...], axis=0)
    precond = []
    for n in range(n_trial):
        if n % half_trials == 0:
            summed = jnp.sum(incoming[n // half_trials].astype(f32), axis=0)
        at = (n % half_trials) * rows
        own = x_ref[n]
        sigma = diagonal * own + summed[at : at + rows, :n_virt]
        sigma_ref[n] = sigma
        omega = sums[n : n + 1, :1] / (sums[n_trial + n : n_trial + n + 1, :1] + 1e-06)
        resid = sigma - omega * own
        precond.append(resid / jnp.maximum(jnp.abs(diagonal - omega), 1.0))
        norms_out[n : n + 1, :] = jnp.broadcast_to(whole(precond[n] * precond[n]), (1, lanes))
    each(lambda step: norm_copy(step).start())
    norms_in[me] = norms_out[...]
    each(lambda step: norm_copy(step).wait_recv())
    norms = jnp.sum(norms_in[...], axis=0)
    count = float(n_occ * n_virt)
    for n in range(n_trial):
        update_ref[n] = precond[n] * lax.rsqrt(norms[n : n + 1, :1] / count + 1e-06)

    block_copy(me, pair, 1).wait_send()
    for step in chip_steps:
        direct_copy(step).wait_send()
        passed_copy(step).wait_send()
    for half in range(2):
        each(lambda step, half=half: sum_copy(half, step).wait_send())
    each(lambda step: scalar_copy(step).wait_send())
    each(lambda step: norm_copy(step).wait_send())


def hand_over(sigma_in, update_in, sigma_ref, update_ref):
    sigma_ref[...] = sigma_in[...]
    update_ref[...] = update_in[...]


def on_device(n_dev, trial_vecs, occ_energy, vir_energy, coul_ov, exch_oo, exch_vv):
    n_trial, rows, n_virt = trial_vecs.shape
    aux_local, n_occ, _ = exch_oo.shape
    width = -(-n_virt // 128) * 128
    half_rows = n_trial // 2 * rows
    group = math.gcd(aux_local // 2, 8)
    vmem = pl.BlockSpec(memory_space=pltpu.VMEM)
    anywhere = pl.BlockSpec(memory_space=pl.ANY)
    out = jax.ShapeDtypeStruct(trial_vecs.shape, jnp.float32)
    dma = pltpu.SemaphoreType.DMA
    sigma, update = pl.pallas_call(
        functools.partial(sigma_kernel, n_dev, group),
        out_shape=(out, out),
        in_specs=[vmem] * 3 + [anywhere] * 3,
        out_specs=(vmem, vmem),
        scratch_shapes=[
            pltpu.VMEM((aux_local, n_virt, n_occ), jnp.bfloat16),
            pltpu.VMEM((aux_local, n_occ, n_occ), jnp.bfloat16),
            pltpu.VMEM((aux_local, n_virt, n_virt), jnp.bfloat16),
            pltpu.VMEM((n_trial * rows, width), jnp.float32),
            pltpu.VMEM((n_dev, n_trial * rows, width), jnp.bfloat16),
            pltpu.VMEM((width, n_trial * n_occ), jnp.bfloat16),
            pltpu.VMEM((n_trial, width, n_occ), jnp.float32),
            pltpu.VMEM((2, n_dev, half_rows, width), jnp.bfloat16),
            pltpu.VMEM((2, n_dev, half_rows, width), jnp.bfloat16),
            pltpu.VMEM((2 * n_trial, 128), jnp.float32),
            pltpu.VMEM((n_dev, 2 * n_trial, 128), jnp.float32),
            pltpu.VMEM((2 * n_trial, 128), jnp.float32),
            pltpu.VMEM((n_dev, 2 * n_trial, 128), jnp.float32),
            pltpu.VMEM((group * n_virt, n_trial // 2 * n_occ), jnp.bfloat16),
            pltpu.VMEM((group * n_virt, n_trial // 2 * n_occ), jnp.bfloat16),
            pltpu.VMEM((n_virt * n_occ // 16, aux_local * 16), jnp.bfloat16),
            pltpu.VMEM((aux_local * n_occ, n_occ), jnp.bfloat16),
            dma((3,)),
            dma((n_dev,)),
            dma((n_dev,)),
            dma((2, n_dev)),
            dma((2, n_dev)),
            dma((n_dev,)),
            dma((n_dev,)),
            dma((n_dev,)),
            dma((n_dev,)),
        ],
        compiler_params=pltpu.CompilerParams(
            collective_id=0, has_side_effects=True, vmem_limit_bytes=56 * 1024 * 1024
        ),
    )(
        trial_vecs,
        occ_energy[None, :],
        vir_energy[None, :],
        coul_ov.transpose(0, 2, 1),
        exch_oo,
        exch_vv,
    )
    return pl.pallas_call(
        hand_over, out_shape=(out, out), in_specs=[vmem] * 2, out_specs=(vmem, vmem)
    )(sigma, update)


def contract(rows_x, coul_ov, exch_oo, exch_vv):
    aux_coef = jnp.einsum("pia,nia->np", coul_ov, rows_x, preferred_element_type=jnp.float32)
    coulomb = jnp.einsum(
        "pia,np->nia", coul_ov, aux_coef.astype(jnp.bfloat16), preferred_element_type=jnp.float32
    )
    aux_local, n_occ, _ = exch_oo.shape
    n_virt = exch_vv.shape[1]
    group_size = math.gcd(aux_local, 16)
    vv_groups = exch_vv.reshape(aux_local // group_size, group_size, n_virt, n_virt)
    oo_groups = exch_oo.reshape(aux_local // group_size, group_size, n_occ, n_occ)

    def advance(running, parts_pair):
        vv_part, oo_part = parts_pair
        halfway = jnp.einsum(
            "pab,njb->pnja", vv_part, rows_x, preferred_element_type=jnp.float32
        ).astype(jnp.bfloat16)
        return (
            running
            + jnp.einsum("pij,pnja->nia", oo_part, halfway, preferred_element_type=jnp.float32),
            None,
        )

    exchange, _ = lax.scan(advance, jnp.zeros(rows_x.shape, jnp.float32), (vv_groups, oo_groups))
    return 2.0 * coulomb - exchange


def on_device_plain(trial_vecs, occ_energy, vir_energy, coul_ov, exch_oo, exch_vv):
    local_rows = trial_vecs.shape[1]
    n_occ, n_virt = coul_ov.shape[1:]
    row_start = lax.axis_index("aux") * local_rows
    rows_x = lax.all_gather(trial_vecs.astype(jnp.bfloat16), "aux", axis=1, tiled=True)
    summed = lax.psum_scatter(
        contract(rows_x, coul_ov, exch_oo, exch_vv), "aux", scatter_dimension=1, tiled=True
    )
    occ_rows = lax.dynamic_slice_in_dim(occ_energy, row_start, local_rows, 0)
    diagonal = vir_energy[None, :] - occ_rows[:, None]
    sigma = diagonal[None] * trial_vecs + summed
    sums = lax.psum(
        jnp.stack([jnp.sum(trial_vecs * sigma, (1, 2)), jnp.sum(trial_vecs * trial_vecs, (1, 2))]),
        "aux",
    )
    omega = (sums[0] / (sums[1] + 1e-06))[:, None, None]
    precond = (sigma - omega * trial_vecs) / jnp.maximum(jnp.abs(diagonal[None] - omega), 1.0)
    squares = lax.psum(jnp.sum(precond * precond, axis=(1, 2)), "aux") / (n_occ * n_virt)
    return sigma, precond * lax.rsqrt(squares + 1e-06)[:, None, None]


def solution(mesh):
    n_dev = mesh.shape["aux"]

    def body(trial_vecs, occ_energy, vir_energy, coul_ov, exch_oo, exch_vv):
        n_trial, rows, n_virt = trial_vecs.shape
        aux_local, n_occ, _ = exch_oo.shape
        tiled = (
            n_trial % 4 == 0
            and rows % 8 == 0
            and n_occ % 128 == 0
            and n_virt % 32 == 0
            and aux_local % 16 == 0
            and n_dev % 2 == 0
        )
        args = (trial_vecs, occ_energy, vir_energy, coul_ov, exch_oo, exch_vv)
        return on_device(n_dev, *args) if tiled else on_device_plain(*args)

    in_specs = (
        P("geom", "aux", None),
        P("geom"),
        P("geom"),
        P(("geom", "aux"), None, None),
        P(("geom", "aux"), None, None),
        P(("geom", "aux"), None, None),
    )
    out_specs = (P("geom", "aux", None), P("geom", "aux", None))
    return jax.shard_map(body, mesh=mesh, in_specs=in_specs, out_specs=out_specs, check_vma=False)
```

```python
import functools
import math

import jax
import jax.numpy as jnp
from jax import lax
from jax.experimental import pallas as pl
from jax.experimental.pallas import tpu as pltpu
from jax.sharding import PartitionSpec as P

MESH = pl.DeviceIdType.MESH


def sigma_kernel(
    n_dev,
    group,
    x_ref,
    occ_ref,
    vir_ref,
    coul_hbm,
    oo_hbm,
    vv_hbm,
    sigma_ref,
    update_ref,
    coul,
    oo,
    vv,
    x_pad,
    gathered,
    x_t,
    total,
    outgoing,
    incoming,
    scalars_out,
    scalars_in,
    norms_out,
    norms_in,
    halfway_a,
    halfway_b,
    coul_t,
    oo_t,
    load_sem,
    gather_send,
    gather_recv,
    sum_send,
    sum_recv,
    scalar_send,
    scalar_recv,
    norm_send,
    norm_recv,
):
    me = lax.axis_index("aux")
    n_trial, rows, n_virt = x_ref.shape
    aux_local, n_occ, _ = oo.shape
    width = x_pad.shape[1]
    half_trials = n_trial // 2
    half_cols = half_trials * n_occ
    f32, bf16 = jnp.float32, jnp.bfloat16

    loads = [
        pltpu.make_async_copy(source, target, load_sem.at[slot])
        for slot, (source, target) in enumerate(((coul_hbm, coul), (oo_hbm, oo), (vv_hbm, vv)))
    ]
    for load in loads:
        load.start()

    barrier = pltpu.get_barrier_semaphore()

    def greet(step, carry):
        pl.semaphore_signal(
            barrier, inc=1, device_id={"aux": lax.rem(me + step, n_dev)}, device_id_type=MESH
        )
        return carry

    lax.fori_loop(1, n_dev, greet, 0)

    x_pad[...] = jnp.zeros_like(x_pad)
    x_pad[:, :n_virt] = x_ref[...].reshape(n_trial * rows, n_virt)
    gathered[me] = x_pad[...].astype(bf16)
    pl.semaphore_wait(barrier, n_dev - 1)

    def to_peer(source, target, send_sem, recv_sem, step):
        return pltpu.make_async_remote_copy(
            src_ref=source,
            dst_ref=target,
            send_sem=send_sem.at[step],
            recv_sem=recv_sem.at[step],
            device_id={"aux": lax.rem(me + step, n_dev)},
            device_id_type=MESH,
        )

    pair = me + 1 - 2 * lax.rem(me, 2)
    chip_steps = sorted(range(2, n_dev, 2), key=lambda step: -min(step, n_dev - step))

    def block_copy(owner, peer, sem_at):
        return pltpu.make_async_remote_copy(
            src_ref=gathered.at[owner],
            dst_ref=gathered.at[owner],
            send_sem=gather_send.at[sem_at],
            recv_sem=gather_recv.at[sem_at],
            device_id={"aux": peer},
            device_id_type=MESH,
        )

    def direct_copy(step):
        return block_copy(me, lax.rem(me + step, n_dev), step)

    def passed_copy(step):
        return block_copy(lax.rem(me + n_dev - step, n_dev), pair, step + 1)

    def sum_copy(half, step):
        peer = lax.rem(me + step, n_dev)
        return to_peer(
            outgoing.at[half, peer], incoming.at[half, me], sum_send.at[half], sum_recv.at[half], step
        )

    def scalar_copy(step):
        return to_peer(scalars_out, scalars_in.at[me], scalar_send, scalar_recv, step)

    def norm_copy(step):
        return to_peer(norms_out, norms_in.at[me], norm_send, norm_recv, step)

    def each(action):
        def body(step, carry):
            action(step)
            return carry

        lax.fori_loop(1, n_dev, body, 0)

    for step in chip_steps:
        direct_copy(step).start()
    block_copy(me, pair, 1).start()

    block = 16
    tiles = n_virt // block
    z_rows, z_cols = n_trial * block, aux_local * block
    loads[0].wait()
    for t in range(tiles):
        coul_t[t * n_occ : (t + 1) * n_occ, :] = (
            coul[:, t * block : (t + 1) * block, :].reshape(z_cols, n_occ).T
        )

    def pass_on(steps):
        for step in steps:
            direct_copy(step).wait_recv()
            passed_copy(step).start()

    near_first = chip_steps[::-1]
    pass_on(near_first[: len(near_first) // 2])
    loads[1].wait()

    def turn(index, carry):
        for p in range(group):
            at = index * group + p
            oo_t[pl.ds(at * n_occ, n_occ), :] = oo[at].T
        return carry

    lax.fori_loop(0, aux_local // group, turn, 0)
    pass_on(near_first[len(near_first) // 2 :])
    loads[2].wait()
    block_copy(me, pair, 1).wait_recv()
    for step in reversed(chip_steps):
        passed_copy(step).wait_recv()

    wide = gathered[...].astype(f32).reshape(n_dev, n_trial, rows, width)
    for n in range(n_trial):
        x_t[:, n * n_occ : (n + 1) * n_occ] = (
            wide[:, n].reshape(n_occ, width).T.astype(bf16)
        )

    def first_step(half, index, slot):
        slot[...] = jnp.dot(
            vv[pl.ds(index * group, group)].reshape(group * n_virt, n_virt),
            x_t[:n_virt, half * half_cols : (half + 1) * half_cols],
            preferred_element_type=f32,
        ).astype(bf16)

    first_step(0, 0, halfway_a)

    left = jnp.concatenate(
        [
            jnp.concatenate(
                [
                    x_t[t * block : (t + 1) * block, n * n_occ : (n + 1) * n_occ]
                    for n in range(n_trial)
                ],
                axis=0,
            )
            for t in range(tiles)
        ],
        axis=1,
    )
    z = jnp.dot(left, coul_t[...], preferred_element_type=f32)
    same = (
        lax.broadcasted_iota(jnp.int32, (z_rows, z_cols), 0) % block
        == lax.broadcasted_iota(jnp.int32, (z_rows, z_cols), 1) % block
    )
    z = jnp.sum(jnp.where(same, z, 0.0).reshape(n_trial, block, z_cols), axis=1)
    lanes = 128
    chunks = z_cols // lanes
    ones = (
        lax.broadcasted_iota(jnp.int32, (lanes, lanes), 0) // block
        == lax.broadcasted_iota(jnp.int32, (lanes, lanes), 1) // block
    ).astype(bf16)
    z = jnp.concatenate([z[:, c * lanes : (c + 1) * lanes] for c in range(chunks)], axis=0)
    coef = jnp.zeros_like(z)
    for _ in range(3):
        piece = z.astype(bf16)
        z = z - piece.astype(f32)
        coef = coef + jnp.dot(piece, ones, preferred_element_type=f32)
    coef = jnp.concatenate(
        [coef[c * n_trial : (c + 1) * n_trial] for c in range(chunks)], axis=1
    )
    coef = jnp.broadcast_to(coef[:, None, :], (n_trial, block, z_cols)).reshape(z_rows, z_cols)
    spread = jnp.where(same, coef, 0.0).astype(bf16)
    total[...] = jnp.zeros_like(total)
    for pair in range(tiles // 2):
        right = jnp.concatenate(
            [
                coul[:, (2 * pair + t) * block : (2 * pair + t + 1) * block, :].reshape(z_cols, n_occ)
                for t in range(2)
            ],
            axis=1,
        )
        part = 2.0 * jnp.dot(spread, right, preferred_element_type=f32)
        for t in range(2):
            for n in range(n_trial):
                total[n, (2 * pair + t) * block : (2 * pair + t + 1) * block, :] = part[
                    n * block : (n + 1) * block, t * n_occ : (t + 1) * n_occ
                ]

    for half in range(2):
        def second_step(index, slot, half=half):
            left = jnp.concatenate(
                [
                    jnp.concatenate(
                        [
                            slot[p * n_virt : (p + 1) * n_virt, n * n_occ : (n + 1) * n_occ]
                            for p in range(group)
                        ],
                        axis=1,
                    )
                    for n in range(half_trials)
                ],
                axis=0,
            )
            right = oo_t[pl.ds(index * (group * n_occ), group * n_occ), :]
            part = jnp.dot(left, right, preferred_element_type=f32)
            for n in range(half_trials):
                at = half * half_trials + n
                total[at, :n_virt, :] = (
                    total[at, :n_virt, :] - part[n * n_virt : (n + 1) * n_virt, :]
                )

        def exchange(index, carry, half=half):
            first_step(half, 2 * index + 1, halfway_b)
            second_step(2 * index, halfway_a)
            first_step(half, 2 * index + 2, halfway_a)
            second_step(2 * index + 1, halfway_b)
            return carry

        groups = aux_local // group
        lax.fori_loop(0, groups // 2 - 1, exchange, 0)
        first_step(half, groups - 1, halfway_b)
        second_step(groups - 2, halfway_a)
        if half == 0:
            first_step(1, 0, halfway_a)
        second_step(groups - 1, halfway_b)
        outgoing[half] = jnp.concatenate(
            [
                total[half * half_trials + n].T.reshape(n_dev, rows, width)
                for n in range(half_trials)
            ],
            axis=1,
        ).astype(bf16)
        each(lambda step, half=half: sum_copy(half, step).start())
        incoming[half, me] = outgoing[half, me]

    row_at = lax.broadcasted_iota(jnp.int32, (rows, n_occ), 0) + me * rows
    col_at = lax.broadcasted_iota(jnp.int32, (rows, n_occ), 1)
    occ_rows = jnp.sum(jnp.where(row_at == col_at, occ_ref[...], 0.0), axis=1, keepdims=True)
    diagonal = vir_ref[...] - occ_rows

    def whole(value):
        return jnp.sum(jnp.sum(value, axis=0, keepdims=True), axis=1, keepdims=True)

    numer, denom = [], []
    for n in range(n_trial):
        own = x_ref[n]
        square = own * own
        x_n = x_t[:, n * n_occ : (n + 1) * n_occ].astype(f32)
        numer.append(whole(x_n * total[n]) + whole(diagonal * square))
        denom.append(whole(square))
    for n in range(n_trial):
        scalars_out[n : n + 1, :] = jnp.broadcast_to(numer[n], (1, lanes))
        scalars_out[n_trial + n : n_trial + n + 1, :] = jnp.broadcast_to(denom[n], (1, lanes))
    each(lambda step: scalar_copy(step).start())
    scalars_in[me] = scalars_out[...]

    summed = []
    for half in range(2):
        each(lambda step, half=half: sum_copy(half, step).wait_recv())
        summed.append(jnp.sum(incoming[half].astype(f32), axis=0))
    each(lambda step: scalar_copy(step).wait_recv())

    sums = jnp.sum(scalars_in[...], axis=0)
    precond = []
    for n in range(n_trial):
        at = (n % half_trials) * rows
        own = x_ref[n]
        sigma = diagonal * own + summed[n // half_trials][at : at + rows, :n_virt]
        sigma_ref[n] = sigma
        omega = sums[n : n + 1, :1] / (sums[n_trial + n : n_trial + n + 1, :1] + 1e-06)
        resid = sigma - omega * own
        precond.append(resid / jnp.maximum(jnp.abs(diagonal - omega), 1.0))
        norms_out[n : n + 1, :] = jnp.broadcast_to(whole(precond[n] * precond[n]), (1, lanes))
    each(lambda step: norm_copy(step).start())
    norms_in[me] = norms_out[...]
    each(lambda step: norm_copy(step).wait_recv())
    norms = jnp.sum(norms_in[...], axis=0)
    count = float(n_occ * n_virt)
    for n in range(n_trial):
        update_ref[n] = precond[n] * lax.rsqrt(norms[n : n + 1, :1] / count + 1e-06)

    block_copy(me, pair, 1).wait_send()
    for step in chip_steps:
        direct_copy(step).wait_send()
        passed_copy(step).wait_send()
    for half in range(2):
        each(lambda step, half=half: sum_copy(half, step).wait_send())
    each(lambda step: scalar_copy(step).wait_send())
    each(lambda step: norm_copy(step).wait_send())


def hand_over(sigma_in, update_in, sigma_ref, update_ref):
    sigma_ref[...] = sigma_in[...]
    update_ref[...] = update_in[...]


def on_device(n_dev, trial_vecs, occ_energy, vir_energy, coul_ov, exch_oo, exch_vv):
    n_trial, rows, n_virt = trial_vecs.shape
    aux_local, n_occ, _ = exch_oo.shape
    width = -(-n_virt // 128) * 128
    half_rows = n_trial // 2 * rows
    group = math.gcd(aux_local // 2, 8)
    vmem = pl.BlockSpec(memory_space=pltpu.VMEM)
    anywhere = pl.BlockSpec(memory_space=pl.ANY)
    out = jax.ShapeDtypeStruct(trial_vecs.shape, jnp.float32)
    dma = pltpu.SemaphoreType.DMA
    sigma, update = pl.pallas_call(
        functools.partial(sigma_kernel, n_dev, group),
        out_shape=(out, out),
        in_specs=[vmem] * 3 + [anywhere] * 3,
        out_specs=(vmem, vmem),
        scratch_shapes=[
            pltpu.VMEM((aux_local, n_virt, n_occ), jnp.bfloat16),
            pltpu.VMEM((aux_local, n_occ, n_occ), jnp.bfloat16),
            pltpu.VMEM((aux_local, n_virt, n_virt), jnp.bfloat16),
            pltpu.VMEM((n_trial * rows, width), jnp.float32),
            pltpu.VMEM((n_dev, n_trial * rows, width), jnp.bfloat16),
            pltpu.VMEM((width, n_trial * n_occ), jnp.bfloat16),
            pltpu.VMEM((n_trial, width, n_occ), jnp.float32),
            pltpu.VMEM((2, n_dev, half_rows, width), jnp.bfloat16),
            pltpu.VMEM((2, n_dev, half_rows, width), jnp.bfloat16),
            pltpu.VMEM((2 * n_trial, 128), jnp.float32),
            pltpu.VMEM((n_dev, 2 * n_trial, 128), jnp.float32),
            pltpu.VMEM((2 * n_trial, 128), jnp.float32),
            pltpu.VMEM((n_dev, 2 * n_trial, 128), jnp.float32),
            pltpu.VMEM((group * n_virt, n_trial // 2 * n_occ), jnp.bfloat16),
            pltpu.VMEM((group * n_virt, n_trial // 2 * n_occ), jnp.bfloat16),
            pltpu.VMEM((n_virt * n_occ // 16, aux_local * 16), jnp.bfloat16),
            pltpu.VMEM((aux_local * n_occ, n_occ), jnp.bfloat16),
            dma((3,)),
            dma((n_dev,)),
            dma((n_dev,)),
            dma((2, n_dev)),
            dma((2, n_dev)),
            dma((n_dev,)),
            dma((n_dev,)),
            dma((n_dev,)),
            dma((n_dev,)),
        ],
        compiler_params=pltpu.CompilerParams(
            collective_id=0, has_side_effects=True, vmem_limit_bytes=56 * 1024 * 1024
        ),
    )(
        trial_vecs,
        occ_energy[None, :],
        vir_energy[None, :],
        coul_ov.transpose(0, 2, 1),
        exch_oo,
        exch_vv,
    )
    return pl.pallas_call(
        hand_over, out_shape=(out, out), in_specs=[vmem] * 2, out_specs=(vmem, vmem)
    )(sigma, update)


def contract(rows_x, coul_ov, exch_oo, exch_vv):
    aux_coef = jnp.einsum("pia,nia->np", coul_ov, rows_x, preferred_element_type=jnp.float32)
    coulomb = jnp.einsum(
        "pia,np->nia", coul_ov, aux_coef.astype(jnp.bfloat16), preferred_element_type=jnp.float32
    )
    aux_local, n_occ, _ = exch_oo.shape
    n_virt = exch_vv.shape[1]
    group_size = math.gcd(aux_local, 16)
    vv_groups = exch_vv.reshape(aux_local // group_size, group_size, n_virt, n_virt)
    oo_groups = exch_oo.reshape(aux_local // group_size, group_size, n_occ, n_occ)

    def advance(running, parts_pair):
        vv_part, oo_part = parts_pair
        halfway = jnp.einsum(
            "pab,njb->pnja", vv_part, rows_x, preferred_element_type=jnp.float32
        ).astype(jnp.bfloat16)
        return (
            running
            + jnp.einsum("pij,pnja->nia", oo_part, halfway, preferred_element_type=jnp.float32),
            None,
        )

    exchange, _ = lax.scan(advance, jnp.zeros(rows_x.shape, jnp.float32), (vv_groups, oo_groups))
    return 2.0 * coulomb - exchange


def on_device_plain(trial_vecs, occ_energy, vir_energy, coul_ov, exch_oo, exch_vv):
    local_rows = trial_vecs.shape[1]
    n_occ, n_virt = coul_ov.shape[1:]
    row_start = lax.axis_index("aux") * local_rows
    rows_x = lax.all_gather(trial_vecs.astype(jnp.bfloat16), "aux", axis=1, tiled=True)
    summed = lax.psum_scatter(
        contract(rows_x, coul_ov, exch_oo, exch_vv), "aux", scatter_dimension=1, tiled=True
    )
    occ_rows = lax.dynamic_slice_in_dim(occ_energy, row_start, local_rows, 0)
    diagonal = vir_energy[None, :] - occ_rows[:, None]
    sigma = diagonal[None] * trial_vecs + summed
    sums = lax.psum(
        jnp.stack([jnp.sum(trial_vecs * sigma, (1, 2)), jnp.sum(trial_vecs * trial_vecs, (1, 2))]),
        "aux",
    )
    omega = (sums[0] / (sums[1] + 1e-06))[:, None, None]
    precond = (sigma - omega * trial_vecs) / jnp.maximum(jnp.abs(diagonal[None] - omega), 1.0)
    squares = lax.psum(jnp.sum(precond * precond, axis=(1, 2)), "aux") / (n_occ * n_virt)
    return sigma, precond * lax.rsqrt(squares + 1e-06)[:, None, None]


def solution(mesh):
    n_dev = mesh.shape["aux"]

    def body(trial_vecs, occ_energy, vir_energy, coul_ov, exch_oo, exch_vv):
        n_trial, rows, n_virt = trial_vecs.shape
        aux_local, n_occ, _ = exch_oo.shape
        tiled = (
            n_trial % 4 == 0
            and rows % 8 == 0
            and n_occ % 128 == 0
            and n_virt % 32 == 0
            and aux_local % 16 == 0
            and n_dev % 2 == 0
        )
        args = (trial_vecs, occ_energy, vir_energy, coul_ov, exch_oo, exch_vv)
        return on_device(n_dev, *args) if tiled else on_device_plain(*args)

    in_specs = (
        P("geom", "aux", None),
        P("geom"),
        P("geom"),
        P(("geom", "aux"), None, None),
        P(("geom", "aux"), None, None),
        P(("geom", "aux"), None, None),
    )
    out_specs = (P("geom", "aux", None), P("geom", "aux", None))
    return jax.shard_map(body, mesh=mesh, in_specs=in_specs, out_specs=out_specs, check_vma=False)
```

```python
import functools
import math

import jax
import jax.numpy as jnp
from jax import lax
from jax.experimental import pallas as pl
from jax.experimental.pallas import tpu as pltpu
from jax.sharding import PartitionSpec as P

MESH = pl.DeviceIdType.MESH


def sigma_kernel(
    n_dev,
    group,
    x_ref,
    occ_ref,
    vir_ref,
    coul_hbm,
    oo_hbm,
    vv_hbm,
    sigma_ref,
    update_ref,
    coul,
    oo,
    vv,
    x_pad,
    gathered,
    x_t,
    total,
    outgoing,
    incoming,
    scalars_out,
    scalars_in,
    norms_out,
    norms_in,
    halfway_a,
    halfway_b,
    coul_t,
    oo_t,
    load_sem,
    gather_send,
    gather_recv,
    sum_send,
    sum_recv,
    scalar_send,
    scalar_recv,
    norm_send,
    norm_recv,
):
    me = lax.axis_index("aux")
    n_trial, rows, n_virt = x_ref.shape
    aux_local, n_occ, _ = oo.shape
    width = x_pad.shape[1]
    half_trials = n_trial // 2
    half_cols = half_trials * n_occ
    lanes = 128
    f32, bf16 = jnp.float32, jnp.bfloat16

    loads = [
        pltpu.make_async_copy(source, target, load_sem.at[slot])
        for slot, (source, target) in enumerate(((oo_hbm, oo), (coul_hbm, coul), (vv_hbm, vv)))
    ]
    for load in loads:
        load.start()

    barrier = pltpu.get_barrier_semaphore()

    def greet(step, carry):
        pl.semaphore_signal(
            barrier, inc=1, device_id={"aux": lax.rem(me + step, n_dev)}, device_id_type=MESH
        )
        return carry

    lax.fori_loop(1, n_dev, greet, 0)

    x_pad[...] = jnp.zeros_like(x_pad)
    x_pad[:, :n_virt] = x_ref[...].reshape(n_trial * rows, n_virt)
    half_rows = half_trials * rows
    for half in range(2):
        gathered[half, me] = x_pad[half * half_rows : (half + 1) * half_rows].astype(bf16)
    pl.semaphore_wait(barrier, n_dev - 1)

    def to_peer(source, target, send_sem, recv_sem, step):
        return pltpu.make_async_remote_copy(
            src_ref=source,
            dst_ref=target,
            send_sem=send_sem.at[step],
            recv_sem=recv_sem.at[step],
            device_id={"aux": lax.rem(me + step, n_dev)},
            device_id_type=MESH,
        )

    pair = me + 1 - 2 * lax.rem(me, 2)
    chip_steps = sorted(range(2, n_dev, 2), key=lambda step: -min(step, n_dev - step))

    def block_copy(half, owner, peer, sem_at):
        return pltpu.make_async_remote_copy(
            src_ref=gathered.at[half, owner],
            dst_ref=gathered.at[half, owner],
            send_sem=gather_send.at[half, sem_at],
            recv_sem=gather_recv.at[half, sem_at],
            device_id={"aux": peer},
            device_id_type=MESH,
        )

    def pair_copy(half):
        return block_copy(half, me, pair, 1)

    def direct_copy(half, step):
        return block_copy(half, me, lax.rem(me + step, n_dev), step)

    def passed_copy(half, step):
        return block_copy(half, lax.rem(me + n_dev - step, n_dev), pair, step + 1)

    def pass_on(half):
        for step in reversed(chip_steps):
            direct_copy(half, step).wait_recv()
            passed_copy(half, step).start()

    def take_in(half):
        pair_copy(half).wait_recv()
        for step in reversed(chip_steps):
            passed_copy(half, step).wait_recv()
        wide = gathered[half].astype(f32).reshape(n_dev, half_trials, rows, width)
        for n in range(half_trials):
            at = half * half_trials + n
            x_t[:, at * n_occ : (at + 1) * n_occ] = wide[:, n].reshape(n_occ, width).T.astype(bf16)

    def sum_copy(half, step):
        peer = lax.rem(me + step, n_dev)
        return to_peer(
            outgoing.at[half, peer], incoming.at[half, me], sum_send.at[half], sum_recv.at[half], step
        )

    def scalar_copy(step):
        return to_peer(scalars_out, scalars_in.at[me], scalar_send, scalar_recv, step)

    def norm_copy(step):
        return to_peer(norms_out, norms_in.at[me], norm_send, norm_recv, step)

    def each(action):
        def body(step, carry):
            action(step)
            return carry

        lax.fori_loop(1, n_dev, body, 0)

    for half in range(2):
        for step in chip_steps:
            direct_copy(half, step).start()
        pair_copy(half).start()

    block = 16
    tiles = n_virt // block
    z_rows, z_cols = n_trial * block, aux_local * block
    loads[0].wait()

    def turn(index, carry):
        for p in range(group):
            at = index * group + p
            oo_t[pl.ds(at * n_occ, n_occ), :] = oo[at].T
        return carry

    lax.fori_loop(0, aux_local // group, turn, 0)
    loads[1].wait()
    for t in range(tiles):
        coul_t[t * n_occ : (t + 1) * n_occ, :] = (
            coul[:, t * block : (t + 1) * block, :].reshape(z_cols, n_occ).T
        )
    loads[2].wait()
    pass_on(0)
    take_in(0)
    total[...] = jnp.zeros_like(total)

    def first_step(half, index, slot):
        slot[...] = jnp.dot(
            vv[pl.ds(index * group, group)].reshape(group * n_virt, n_virt),
            x_t[:n_virt, half * half_cols : (half + 1) * half_cols],
            preferred_element_type=f32,
        ).astype(bf16)

    def add_coulomb():
        left = jnp.concatenate(
            [
                jnp.concatenate(
                    [
                        x_t[t * block : (t + 1) * block, n * n_occ : (n + 1) * n_occ]
                        for n in range(n_trial)
                    ],
                    axis=0,
                )
                for t in range(tiles)
            ],
            axis=1,
        )
        z = jnp.dot(left, coul_t[...], preferred_element_type=f32)
        same = (
            lax.broadcasted_iota(jnp.int32, (z_rows, z_cols), 0) % block
            == lax.broadcasted_iota(jnp.int32, (z_rows, z_cols), 1) % block
        )
        z = jnp.sum(jnp.where(same, z, 0.0).reshape(n_trial, block, z_cols), axis=1)
        chunks = z_cols // lanes
        ones = (
            lax.broadcasted_iota(jnp.int32, (lanes, lanes), 0) // block
            == lax.broadcasted_iota(jnp.int32, (lanes, lanes), 1) // block
        ).astype(bf16)
        z = jnp.concatenate([z[:, c * lanes : (c + 1) * lanes] for c in range(chunks)], axis=0)
        coef = jnp.zeros_like(z)
        for _ in range(3):
            piece = z.astype(bf16)
            z = z - piece.astype(f32)
            coef = coef + jnp.dot(piece, ones, preferred_element_type=f32)
        coef = jnp.concatenate(
            [coef[c * n_trial : (c + 1) * n_trial] for c in range(chunks)], axis=1
        )
        coef = jnp.broadcast_to(coef[:, None, :], (n_trial, block, z_cols)).reshape(z_rows, z_cols)
        spread = jnp.where(same, coef, 0.0).astype(bf16)
        for index in range(tiles // 2):
            spans = [slice((2 * index + t) * block, (2 * index + t + 1) * block) for t in range(2)]
            right = jnp.concatenate(
                [coul[:, span, :].reshape(z_cols, n_occ) for span in spans], axis=1
            )
            part = 2.0 * jnp.dot(spread, right, preferred_element_type=f32)
            for t, span in enumerate(spans):
                for n in range(n_trial):
                    total[n, span, :] = (
                        total[n, span, :]
                        + part[n * block : (n + 1) * block, t * n_occ : (t + 1) * n_occ]
                    )

    first_step(0, 0, halfway_a)
    for half in range(2):

        def second_step(index, slot, half=half):
            left = jnp.concatenate(
                [
                    jnp.concatenate(
                        [
                            slot[p * n_virt : (p + 1) * n_virt, n * n_occ : (n + 1) * n_occ]
                            for p in range(group)
                        ],
                        axis=1,
                    )
                    for n in range(half_trials)
                ],
                axis=0,
            )
            right = oo_t[pl.ds(index * (group * n_occ), group * n_occ), :]
            part = jnp.dot(left, right, preferred_element_type=f32)
            for n in range(half_trials):
                at = half * half_trials + n
                total[at, :n_virt, :] = (
                    total[at, :n_virt, :] - part[n * n_virt : (n + 1) * n_virt, :]
                )

        def exchange(index, carry, half=half):
            first_step(half, 2 * index + 1, halfway_b)
            second_step(2 * index, halfway_a)
            first_step(half, 2 * index + 2, halfway_a)
            second_step(2 * index + 1, halfway_b)
            return carry

        groups = aux_local // group
        if half == 0:
            middle = groups // 4
            lax.fori_loop(0, middle, exchange, 0)
            pass_on(1)
            lax.fori_loop(middle, groups // 2 - 1, exchange, 0)
        else:
            lax.fori_loop(0, groups // 2 - 1, exchange, 0)
        first_step(half, groups - 1, halfway_b)
        second_step(groups - 2, halfway_a)
        if half == 0:
            take_in(1)
            first_step(1, 0, halfway_a)
        second_step(groups - 1, halfway_b)
        if half == 0:
            add_coulomb()
        outgoing[half] = jnp.concatenate(
            [
                total[half * half_trials + n].T.reshape(n_dev, rows, width)
                for n in range(half_trials)
            ],
            axis=1,
        ).astype(bf16)
        each(lambda step, half=half: sum_copy(half, step).start())
        incoming[half, me] = outgoing[half, me]

    row_at = lax.broadcasted_iota(jnp.int32, (rows, n_occ), 0) + me * rows
    col_at = lax.broadcasted_iota(jnp.int32, (rows, n_occ), 1)
    occ_rows = jnp.sum(jnp.where(row_at == col_at, occ_ref[...], 0.0), axis=1, keepdims=True)
    diagonal = vir_ref[...] - occ_rows

    def whole(value):
        return jnp.sum(jnp.sum(value, axis=0, keepdims=True), axis=1, keepdims=True)

    numer, denom = [], []
    for n in range(n_trial):
        own = x_ref[n]
        square = own * own
        x_n = x_t[:, n * n_occ : (n + 1) * n_occ].astype(f32)
        numer.append(whole(x_n * total[n]) + whole(diagonal * square))
        denom.append(whole(square))
    for n in range(n_trial):
        scalars_out[n : n + 1, :] = jnp.broadcast_to(numer[n], (1, lanes))
        scalars_out[n_trial + n : n_trial + n + 1, :] = jnp.broadcast_to(denom[n], (1, lanes))
    each(lambda step: scalar_copy(step).start())
    scalars_in[me] = scalars_out[...]

    for half in range(2):
        each(lambda step, half=half: sum_copy(half, step).wait_recv())
    each(lambda step: scalar_copy(step).wait_recv())

    sums = jnp.sum(scalars_in[...], axis=0)
    precond = []
    for n in range(n_trial):
        if n % half_trials == 0:
            summed = jnp.sum(incoming[n // half_trials].astype(f32), axis=0)
        at = (n % half_trials) * rows
        own = x_ref[n]
        sigma = diagonal * own + summed[at : at + rows, :n_virt]
        sigma_ref[n] = sigma
        omega = sums[n : n + 1, :1] / (sums[n_trial + n : n_trial + n + 1, :1] + 1e-06)
        resid = sigma - omega * own
        precond.append(resid / jnp.maximum(jnp.abs(diagonal - omega), 1.0))
        norms_out[n : n + 1, :] = jnp.broadcast_to(whole(precond[n] * precond[n]), (1, lanes))
    each(lambda step: norm_copy(step).start())
    norms_in[me] = norms_out[...]
    each(lambda step: norm_copy(step).wait_recv())
    norms = jnp.sum(norms_in[...], axis=0)
    count = float(n_occ * n_virt)
    for n in range(n_trial):
        update_ref[n] = precond[n] * lax.rsqrt(norms[n : n + 1, :1] / count + 1e-06)

    for half in range(2):
        pair_copy(half).wait_send()
        for step in chip_steps:
            direct_copy(half, step).wait_send()
            passed_copy(half, step).wait_send()
    for half in range(2):
        each(lambda step, half=half: sum_copy(half, step).wait_send())
    each(lambda step: scalar_copy(step).wait_send())
    each(lambda step: norm_copy(step).wait_send())


def hand_over(sigma_in, update_in, sigma_ref, update_ref):
    sigma_ref[...] = sigma_in[...]
    update_ref[...] = update_in[...]


def on_device(n_dev, trial_vecs, occ_energy, vir_energy, coul_ov, exch_oo, exch_vv):
    n_trial, rows, n_virt = trial_vecs.shape
    aux_local, n_occ, _ = exch_oo.shape
    width = -(-n_virt // 128) * 128
    half_rows = n_trial // 2 * rows
    group = math.gcd(aux_local // 2, 8)
    vmem = pl.BlockSpec(memory_space=pltpu.VMEM)
    anywhere = pl.BlockSpec(memory_space=pl.ANY)
    out = jax.ShapeDtypeStruct(trial_vecs.shape, jnp.float32)
    dma = pltpu.SemaphoreType.DMA
    sigma, update = pl.pallas_call(
        functools.partial(sigma_kernel, n_dev, group),
        out_shape=(out, out),
        in_specs=[vmem] * 3 + [anywhere] * 3,
        out_specs=(vmem, vmem),
        scratch_shapes=[
            pltpu.VMEM((aux_local, n_virt, n_occ), jnp.bfloat16),
            pltpu.VMEM((aux_local, n_occ, n_occ), jnp.bfloat16),
            pltpu.VMEM((aux_local, n_virt, n_virt), jnp.bfloat16),
            pltpu.VMEM((n_trial * rows, width), jnp.float32),
            pltpu.VMEM((2, n_dev, half_rows, width), jnp.bfloat16),
            pltpu.VMEM((width, n_trial * n_occ), jnp.bfloat16),
            pltpu.VMEM((n_trial, width, n_occ), jnp.float32),
            pltpu.VMEM((2, n_dev, half_rows, width), jnp.bfloat16),
            pltpu.VMEM((2, n_dev, half_rows, width), jnp.bfloat16),
            pltpu.VMEM((2 * n_trial, 128), jnp.float32),
            pltpu.VMEM((n_dev, 2 * n_trial, 128), jnp.float32),
            pltpu.VMEM((2 * n_trial, 128), jnp.float32),
            pltpu.VMEM((n_dev, 2 * n_trial, 128), jnp.float32),
            pltpu.VMEM((group * n_virt, n_trial // 2 * n_occ), jnp.bfloat16),
            pltpu.VMEM((group * n_virt, n_trial // 2 * n_occ), jnp.bfloat16),
            pltpu.VMEM((n_virt * n_occ // 16, aux_local * 16), jnp.bfloat16),
            pltpu.VMEM((aux_local * n_occ, n_occ), jnp.bfloat16),
            dma((3,)),
            dma((2, n_dev)),
            dma((2, n_dev)),
            dma((2, n_dev)),
            dma((2, n_dev)),
            dma((n_dev,)),
            dma((n_dev,)),
            dma((n_dev,)),
            dma((n_dev,)),
        ],
        compiler_params=pltpu.CompilerParams(
            collective_id=0, has_side_effects=True, vmem_limit_bytes=56 * 1024 * 1024
        ),
    )(
        trial_vecs,
        occ_energy[None, :],
        vir_energy[None, :],
        coul_ov.transpose(0, 2, 1),
        exch_oo,
        exch_vv,
    )
    return pl.pallas_call(
        hand_over, out_shape=(out, out), in_specs=[vmem] * 2, out_specs=(vmem, vmem)
    )(sigma, update)


def contract(rows_x, coul_ov, exch_oo, exch_vv):
    aux_coef = jnp.einsum("pia,nia->np", coul_ov, rows_x, preferred_element_type=jnp.float32)
    coulomb = jnp.einsum(
        "pia,np->nia", coul_ov, aux_coef.astype(jnp.bfloat16), preferred_element_type=jnp.float32
    )
    aux_local, n_occ, _ = exch_oo.shape
    n_virt = exch_vv.shape[1]
    group_size = math.gcd(aux_local, 16)
    vv_groups = exch_vv.reshape(aux_local // group_size, group_size, n_virt, n_virt)
    oo_groups = exch_oo.reshape(aux_local // group_size, group_size, n_occ, n_occ)

    def advance(running, parts_pair):
        vv_part, oo_part = parts_pair
        halfway = jnp.einsum(
            "pab,njb->pnja", vv_part, rows_x, preferred_element_type=jnp.float32
        ).astype(jnp.bfloat16)
        return (
            running
            + jnp.einsum("pij,pnja->nia", oo_part, halfway, preferred_element_type=jnp.float32),
            None,
        )

    exchange, _ = lax.scan(advance, jnp.zeros(rows_x.shape, jnp.float32), (vv_groups, oo_groups))
    return 2.0 * coulomb - exchange


def on_device_plain(trial_vecs, occ_energy, vir_energy, coul_ov, exch_oo, exch_vv):
    local_rows = trial_vecs.shape[1]
    n_occ, n_virt = coul_ov.shape[1:]
    row_start = lax.axis_index("aux") * local_rows
    rows_x = lax.all_gather(trial_vecs.astype(jnp.bfloat16), "aux", axis=1, tiled=True)
    summed = lax.psum_scatter(
        contract(rows_x, coul_ov, exch_oo, exch_vv), "aux", scatter_dimension=1, tiled=True
    )
    occ_rows = lax.dynamic_slice_in_dim(occ_energy, row_start, local_rows, 0)
    diagonal = vir_energy[None, :] - occ_rows[:, None]
    sigma = diagonal[None] * trial_vecs + summed
    sums = lax.psum(
        jnp.stack([jnp.sum(trial_vecs * sigma, (1, 2)), jnp.sum(trial_vecs * trial_vecs, (1, 2))]),
        "aux",
    )
    omega = (sums[0] / (sums[1] + 1e-06))[:, None, None]
    precond = (sigma - omega * trial_vecs) / jnp.maximum(jnp.abs(diagonal[None] - omega), 1.0)
    squares = lax.psum(jnp.sum(precond * precond, axis=(1, 2)), "aux") / (n_occ * n_virt)
    return sigma, precond * lax.rsqrt(squares + 1e-06)[:, None, None]


def solution(mesh):
    n_dev = mesh.shape["aux"]

    def body(trial_vecs, occ_energy, vir_energy, coul_ov, exch_oo, exch_vv):
        n_trial, rows, n_virt = trial_vecs.shape
        aux_local, n_occ, _ = exch_oo.shape
        tiled = (
            n_trial % 4 == 0
            and rows % 8 == 0
            and n_occ % 128 == 0
            and n_virt % 32 == 0
            and aux_local % 16 == 0
            and n_dev % 2 == 0
        )
        args = (trial_vecs, occ_energy, vir_energy, coul_ov, exch_oo, exch_vv)
        return on_device(n_dev, *args) if tiled else on_device_plain(*args)

    in_specs = (
        P("geom", "aux", None),
        P("geom"),
        P("geom"),
        P(("geom", "aux"), None, None),
        P(("geom", "aux"), None, None),
        P(("geom", "aux"), None, None),
    )
    out_specs = (P("geom", "aux", None), P("geom", "aux", None))
    return jax.shard_map(body, mesh=mesh, in_specs=in_specs, out_specs=out_specs, check_vma=False)
```

```python
import functools
import math

import jax
import jax.numpy as jnp
from jax import lax
from jax.experimental import pallas as pl
from jax.experimental.pallas import tpu as pltpu
from jax.sharding import PartitionSpec as P

MESH = pl.DeviceIdType.MESH


def sigma_kernel(
    n_dev,
    group,
    x_ref,
    occ_ref,
    vir_ref,
    coul_hbm,
    oo_hbm,
    vv_hbm,
    sigma_ref,
    update_ref,
    coul,
    oo,
    vv,
    x_pad,
    gathered,
    x_t,
    total,
    outgoing,
    incoming,
    scalars_out,
    scalars_in,
    norms_out,
    norms_in,
    halfway_a,
    halfway_b,
    coul_t,
    oo_t,
    load_sem,
    gather_send,
    gather_recv,
    sum_send,
    sum_recv,
    scalar_send,
    scalar_recv,
    norm_send,
    norm_recv,
):
    me = lax.axis_index("aux")
    n_trial, rows, n_virt = x_ref.shape
    aux_local, n_occ, _ = oo.shape
    width = x_pad.shape[1]
    half_trials = n_trial // 2
    half_cols = half_trials * n_occ
    lanes = 128
    f32, bf16 = jnp.float32, jnp.bfloat16

    loads = [
        pltpu.make_async_copy(source, target, load_sem.at[slot])
        for slot, (source, target) in enumerate(((oo_hbm, oo), (coul_hbm, coul), (vv_hbm, vv)))
    ]
    for load in loads:
        load.start()

    barrier = pltpu.get_barrier_semaphore()

    def greet(step, carry):
        pl.semaphore_signal(
            barrier, inc=1, device_id={"aux": lax.rem(me + step, n_dev)}, device_id_type=MESH
        )
        return carry

    lax.fori_loop(1, n_dev, greet, 0)

    x_pad[...] = jnp.zeros_like(x_pad)
    x_pad[:, :n_virt] = x_ref[...].reshape(n_trial * rows, n_virt)
    half_rows = half_trials * rows
    for half in range(2):
        gathered[half, me] = x_pad[half * half_rows : (half + 1) * half_rows].astype(bf16)
    pl.semaphore_wait(barrier, n_dev - 1)

    def to_peer(source, target, send_sem, recv_sem, step):
        return pltpu.make_async_remote_copy(
            src_ref=source,
            dst_ref=target,
            send_sem=send_sem.at[step],
            recv_sem=recv_sem.at[step],
            device_id={"aux": lax.rem(me + step, n_dev)},
            device_id_type=MESH,
        )

    pair = me + 1 - 2 * lax.rem(me, 2)
    chip_steps = sorted(range(2, n_dev, 2), key=lambda step: -min(step, n_dev - step))

    def block_copy(half, owner, peer, sem_at):
        return pltpu.make_async_remote_copy(
            src_ref=gathered.at[half, owner],
            dst_ref=gathered.at[half, owner],
            send_sem=gather_send.at[half, sem_at],
            recv_sem=gather_recv.at[half, sem_at],
            device_id={"aux": peer},
            device_id_type=MESH,
        )

    def pair_copy(half):
        return block_copy(half, me, pair, 1)

    def direct_copy(half, step):
        return block_copy(half, me, lax.rem(me + step, n_dev), step)

    def passed_copy(half, step):
        return block_copy(half, lax.rem(me + n_dev - step, n_dev), pair, step + 1)

    def pass_on(half):
        for step in reversed(chip_steps):
            direct_copy(half, step).wait_recv()
            passed_copy(half, step).start()

    def take_in(half):
        pair_copy(half).wait_recv()
        for step in reversed(chip_steps):
            passed_copy(half, step).wait_recv()
        wide = gathered[half].astype(f32).reshape(n_dev, half_trials, rows, width)
        for n in range(half_trials):
            at = half * half_trials + n
            x_t[:, at * n_occ : (at + 1) * n_occ] = wide[:, n].reshape(n_occ, width).T.astype(bf16)

    def sum_copy(half, step):
        peer = lax.rem(me + step, n_dev)
        return to_peer(
            outgoing.at[half, peer], incoming.at[half, me], sum_send.at[half], sum_recv.at[half], step
        )

    def scalar_copy(step):
        return to_peer(scalars_out, scalars_in.at[me], scalar_send, scalar_recv, step)

    def norm_copy(step):
        return to_peer(norms_out, norms_in.at[me], norm_send, norm_recv, step)

    def each(action):
        def body(step, carry):
            action(step)
            return carry

        lax.fori_loop(1, n_dev, body, 0)

    for half in range(2):
        for step in chip_steps:
            direct_copy(half, step).start()
        pair_copy(half).start()

    block = 16
    tiles = n_virt // block
    z_rows, z_cols = n_trial * block, aux_local * block
    loads[0].wait()

    def turn(index, carry):
        for p in range(group):
            at = index * group + p
            oo_t[pl.ds(at * n_occ, n_occ), :] = oo[at].T
        return carry

    lax.fori_loop(0, aux_local // group, turn, 0)
    loads[1].wait()
    loads[2].wait()
    pass_on(0)
    take_in(0)
    total[...] = jnp.zeros_like(total)

    def first_step(half, index, slot):
        slot[...] = jnp.dot(
            vv[pl.ds(index * group, group)].reshape(group * n_virt, n_virt),
            x_t[:n_virt, half * half_cols : (half + 1) * half_cols],
            preferred_element_type=f32,
        ).astype(bf16)

    def add_coulomb():
        left = jnp.concatenate(
            [
                jnp.concatenate(
                    [
                        x_t[t * block : (t + 1) * block, n * n_occ : (n + 1) * n_occ]
                        for n in range(n_trial)
                    ],
                    axis=0,
                )
                for t in range(tiles)
            ],
            axis=1,
        )
        z = jnp.dot(left, coul_t[...], preferred_element_type=f32)
        same = (
            lax.broadcasted_iota(jnp.int32, (z_rows, z_cols), 0) % block
            == lax.broadcasted_iota(jnp.int32, (z_rows, z_cols), 1) % block
        )
        z = jnp.sum(jnp.where(same, z, 0.0).reshape(n_trial, block, z_cols), axis=1)
        chunks = z_cols // lanes
        ones = (
            lax.broadcasted_iota(jnp.int32, (lanes, lanes), 0) // block
            == lax.broadcasted_iota(jnp.int32, (lanes, lanes), 1) // block
        ).astype(bf16)
        z = jnp.concatenate([z[:, c * lanes : (c + 1) * lanes] for c in range(chunks)], axis=0)
        coef = jnp.zeros_like(z)
        for _ in range(3):
            piece = z.astype(bf16)
            z = z - piece.astype(f32)
            coef = coef + jnp.dot(piece, ones, preferred_element_type=f32)
        coef = jnp.concatenate(
            [coef[c * n_trial : (c + 1) * n_trial] for c in range(chunks)], axis=1
        )
        coef = jnp.broadcast_to(coef[:, None, :], (n_trial, block, z_cols)).reshape(z_rows, z_cols)
        spread = jnp.where(same, coef, 0.0).astype(bf16)
        for index in range(tiles // 2):
            spans = [slice((2 * index + t) * block, (2 * index + t + 1) * block) for t in range(2)]
            right = jnp.concatenate(
                [coul[:, span, :].reshape(z_cols, n_occ) for span in spans], axis=1
            )
            part = 2.0 * jnp.dot(spread, right, preferred_element_type=f32)
            for t, span in enumerate(spans):
                for n in range(n_trial):
                    total[n, span, :] = (
                        total[n, span, :]
                        + part[n * block : (n + 1) * block, t * n_occ : (t + 1) * n_occ]
                    )

    first_step(0, 0, halfway_a)
    for half in range(2):

        def second_step(index, slot, half=half):
            left = jnp.concatenate(
                [
                    jnp.concatenate(
                        [
                            slot[p * n_virt : (p + 1) * n_virt, n * n_occ : (n + 1) * n_occ]
                            for p in range(group)
                        ],
                        axis=1,
                    )
                    for n in range(half_trials)
                ],
                axis=0,
            )
            right = oo_t[pl.ds(index * (group * n_occ), group * n_occ), :]
            part = jnp.dot(left, right, preferred_element_type=f32)
            for n in range(half_trials):
                at = half * half_trials + n
                total[at, :n_virt, :] = (
                    total[at, :n_virt, :] - part[n * n_virt : (n + 1) * n_virt, :]
                )

        def exchange(index, carry, half=half):
            first_step(half, 2 * index + 1, halfway_b)
            second_step(2 * index, halfway_a)
            first_step(half, 2 * index + 2, halfway_a)
            second_step(2 * index + 1, halfway_b)
            return carry

        groups = aux_local // group
        trips = groups // 2 - 1
        if half == 0:
            share = -(-tiles // trips)

            def exchange_and_turn(index, carry, exchange=exchange, share=share):
                for q in range(share):
                    t = jnp.minimum(index * share + q, tiles - 1)
                    coul_t[pl.ds(t * n_occ, n_occ), :] = (
                        coul[:, pl.ds(t * block, block), :].reshape(z_cols, n_occ).T
                    )
                return exchange(index, carry)

            middle = groups // 4
            lax.fori_loop(0, middle, exchange_and_turn, 0)
            pass_on(1)
            lax.fori_loop(middle, trips, exchange_and_turn, 0)
        else:
            lax.fori_loop(0, trips, exchange, 0)
        first_step(half, groups - 1, halfway_b)
        second_step(groups - 2, halfway_a)
        if half == 0:
            take_in(1)
            first_step(1, 0, halfway_a)
        second_step(groups - 1, halfway_b)
        if half == 0:
            add_coulomb()
        outgoing[half] = jnp.concatenate(
            [
                total[half * half_trials + n].T.reshape(n_dev, rows, width)
                for n in range(half_trials)
            ],
            axis=1,
        ).astype(bf16)
        each(lambda step, half=half: sum_copy(half, step).start())
        incoming[half, me] = outgoing[half, me]

    row_at = lax.broadcasted_iota(jnp.int32, (rows, n_occ), 0) + me * rows
    col_at = lax.broadcasted_iota(jnp.int32, (rows, n_occ), 1)
    occ_rows = jnp.sum(jnp.where(row_at == col_at, occ_ref[...], 0.0), axis=1, keepdims=True)
    diagonal = vir_ref[...] - occ_rows

    def whole(value):
        return jnp.sum(jnp.sum(value, axis=0, keepdims=True), axis=1, keepdims=True)

    numer, denom = [], []
    for n in range(n_trial):
        own = x_ref[n]
        square = own * own
        x_n = x_t[:, n * n_occ : (n + 1) * n_occ].astype(f32)
        numer.append(whole(x_n * total[n]) + whole(diagonal * square))
        denom.append(whole(square))
    for n in range(n_trial):
        scalars_out[n : n + 1, :] = jnp.broadcast_to(numer[n], (1, lanes))
        scalars_out[n_trial + n : n_trial + n + 1, :] = jnp.broadcast_to(denom[n], (1, lanes))
    each(lambda step: scalar_copy(step).start())
    scalars_in[me] = scalars_out[...]

    for half in range(2):
        each(lambda step, half=half: sum_copy(half, step).wait_recv())
    each(lambda step: scalar_copy(step).wait_recv())

    sums = jnp.sum(scalars_in[...], axis=0)
    precond = []
    for n in range(n_trial):
        if n % half_trials == 0:
            summed = jnp.sum(incoming[n // half_trials].astype(f32), axis=0)
        at = (n % half_trials) * rows
        own = x_ref[n]
        sigma = diagonal * own + summed[at : at + rows, :n_virt]
        sigma_ref[n] = sigma
        omega = sums[n : n + 1, :1] / (sums[n_trial + n : n_trial + n + 1, :1] + 1e-06)
        resid = sigma - omega * own
        precond.append(resid / jnp.maximum(jnp.abs(diagonal - omega), 1.0))
        norms_out[n : n + 1, :] = jnp.broadcast_to(whole(precond[n] * precond[n]), (1, lanes))
    each(lambda step: norm_copy(step).start())
    norms_in[me] = norms_out[...]
    each(lambda step: norm_copy(step).wait_recv())
    norms = jnp.sum(norms_in[...], axis=0)
    count = float(n_occ * n_virt)
    for n in range(n_trial):
        update_ref[n] = precond[n] * lax.rsqrt(norms[n : n + 1, :1] / count + 1e-06)

    for half in range(2):
        pair_copy(half).wait_send()
        for step in chip_steps:
            direct_copy(half, step).wait_send()
            passed_copy(half, step).wait_send()
    for half in range(2):
        each(lambda step, half=half: sum_copy(half, step).wait_send())
    each(lambda step: scalar_copy(step).wait_send())
    each(lambda step: norm_copy(step).wait_send())


def hand_over(sigma_in, update_in, sigma_ref, update_ref):
    sigma_ref[...] = sigma_in[...]
    update_ref[...] = update_in[...]


def on_device(n_dev, trial_vecs, occ_energy, vir_energy, coul_ov, exch_oo, exch_vv):
    n_trial, rows, n_virt = trial_vecs.shape
    aux_local, n_occ, _ = exch_oo.shape
    width = -(-n_virt // 128) * 128
    half_rows = n_trial // 2 * rows
    group = math.gcd(aux_local // 2, 8)
    vmem = pl.BlockSpec(memory_space=pltpu.VMEM)
    anywhere = pl.BlockSpec(memory_space=pl.ANY)
    out = jax.ShapeDtypeStruct(trial_vecs.shape, jnp.float32)
    dma = pltpu.SemaphoreType.DMA
    sigma, update = pl.pallas_call(
        functools.partial(sigma_kernel, n_dev, group),
        out_shape=(out, out),
        in_specs=[vmem] * 3 + [anywhere] * 3,
        out_specs=(vmem, vmem),
        scratch_shapes=[
            pltpu.VMEM((aux_local, n_virt, n_occ), jnp.bfloat16),
            pltpu.VMEM((aux_local, n_occ, n_occ), jnp.bfloat16),
            pltpu.VMEM((aux_local, n_virt, n_virt), jnp.bfloat16),
            pltpu.VMEM((n_trial * rows, width), jnp.float32),
            pltpu.VMEM((2, n_dev, half_rows, width), jnp.bfloat16),
            pltpu.VMEM((width, n_trial * n_occ), jnp.bfloat16),
            pltpu.VMEM((n_trial, width, n_occ), jnp.float32),
            pltpu.VMEM((2, n_dev, half_rows, width), jnp.bfloat16),
            pltpu.VMEM((2, n_dev, half_rows, width), jnp.bfloat16),
            pltpu.VMEM((2 * n_trial, 128), jnp.float32),
            pltpu.VMEM((n_dev, 2 * n_trial, 128), jnp.float32),
            pltpu.VMEM((2 * n_trial, 128), jnp.float32),
            pltpu.VMEM((n_dev, 2 * n_trial, 128), jnp.float32),
            pltpu.VMEM((group * n_virt, n_trial // 2 * n_occ), jnp.bfloat16),
            pltpu.VMEM((group * n_virt, n_trial // 2 * n_occ), jnp.bfloat16),
            pltpu.VMEM((n_virt * n_occ // 16, aux_local * 16), jnp.bfloat16),
            pltpu.VMEM((aux_local * n_occ, n_occ), jnp.bfloat16),
            dma((3,)),
            dma((2, n_dev)),
            dma((2, n_dev)),
            dma((2, n_dev)),
            dma((2, n_dev)),
            dma((n_dev,)),
            dma((n_dev,)),
            dma((n_dev,)),
            dma((n_dev,)),
        ],
        compiler_params=pltpu.CompilerParams(
            collective_id=0, has_side_effects=True, vmem_limit_bytes=56 * 1024 * 1024
        ),
    )(
        trial_vecs,
        occ_energy[None, :],
        vir_energy[None, :],
        coul_ov.transpose(0, 2, 1),
        exch_oo,
        exch_vv,
    )
    return pl.pallas_call(
        hand_over, out_shape=(out, out), in_specs=[vmem] * 2, out_specs=(vmem, vmem)
    )(sigma, update)


def contract(rows_x, coul_ov, exch_oo, exch_vv):
    aux_coef = jnp.einsum("pia,nia->np", coul_ov, rows_x, preferred_element_type=jnp.float32)
    coulomb = jnp.einsum(
        "pia,np->nia", coul_ov, aux_coef.astype(jnp.bfloat16), preferred_element_type=jnp.float32
    )
    aux_local, n_occ, _ = exch_oo.shape
    n_virt = exch_vv.shape[1]
    group_size = math.gcd(aux_local, 16)
    vv_groups = exch_vv.reshape(aux_local // group_size, group_size, n_virt, n_virt)
    oo_groups = exch_oo.reshape(aux_local // group_size, group_size, n_occ, n_occ)

    def advance(running, parts_pair):
        vv_part, oo_part = parts_pair
        halfway = jnp.einsum(
            "pab,njb->pnja", vv_part, rows_x, preferred_element_type=jnp.float32
        ).astype(jnp.bfloat16)
        return (
            running
            + jnp.einsum("pij,pnja->nia", oo_part, halfway, preferred_element_type=jnp.float32),
            None,
        )

    exchange, _ = lax.scan(advance, jnp.zeros(rows_x.shape, jnp.float32), (vv_groups, oo_groups))
    return 2.0 * coulomb - exchange


def on_device_plain(trial_vecs, occ_energy, vir_energy, coul_ov, exch_oo, exch_vv):
    local_rows = trial_vecs.shape[1]
    n_occ, n_virt = coul_ov.shape[1:]
    row_start = lax.axis_index("aux") * local_rows
    rows_x = lax.all_gather(trial_vecs.astype(jnp.bfloat16), "aux", axis=1, tiled=True)
    summed = lax.psum_scatter(
        contract(rows_x, coul_ov, exch_oo, exch_vv), "aux", scatter_dimension=1, tiled=True
    )
    occ_rows = lax.dynamic_slice_in_dim(occ_energy, row_start, local_rows, 0)
    diagonal = vir_energy[None, :] - occ_rows[:, None]
    sigma = diagonal[None] * trial_vecs + summed
    sums = lax.psum(
        jnp.stack([jnp.sum(trial_vecs * sigma, (1, 2)), jnp.sum(trial_vecs * trial_vecs, (1, 2))]),
        "aux",
    )
    omega = (sums[0] / (sums[1] + 1e-06))[:, None, None]
    precond = (sigma - omega * trial_vecs) / jnp.maximum(jnp.abs(diagonal[None] - omega), 1.0)
    squares = lax.psum(jnp.sum(precond * precond, axis=(1, 2)), "aux") / (n_occ * n_virt)
    return sigma, precond * lax.rsqrt(squares + 1e-06)[:, None, None]


def solution(mesh):
    n_dev = mesh.shape["aux"]

    def body(trial_vecs, occ_energy, vir_energy, coul_ov, exch_oo, exch_vv):
        n_trial, rows, n_virt = trial_vecs.shape
        aux_local, n_occ, _ = exch_oo.shape
        tiled = (
            n_trial % 4 == 0
            and rows % 8 == 0
            and n_occ % 128 == 0
            and n_virt % 32 == 0
            and aux_local % 16 == 0
            and aux_local >= 32
            and n_dev % 2 == 0
        )
        args = (trial_vecs, occ_energy, vir_energy, coul_ov, exch_oo, exch_vv)
        return on_device(n_dev, *args) if tiled else on_device_plain(*args)

    in_specs = (
        P("geom", "aux", None),
        P("geom"),
        P("geom"),
        P(("geom", "aux"), None, None),
        P(("geom", "aux"), None, None),
        P(("geom", "aux"), None, None),
    )
    out_specs = (P("geom", "aux", None), P("geom", "aux", None))
    return jax.shard_map(body, mesh=mesh, in_specs=in_specs, out_specs=out_specs, check_vma=False)
```

```python
import functools
import math

import jax
import jax.numpy as jnp
from jax import lax
from jax.experimental import pallas as pl
from jax.experimental.pallas import tpu as pltpu
from jax.sharding import PartitionSpec as P

MESH = pl.DeviceIdType.MESH


def sigma_kernel(
    n_dev,
    group,
    x_ref,
    occ_ref,
    vir_ref,
    coul_hbm,
    oo_hbm,
    vv_hbm,
    sigma_ref,
    update_ref,
    coul,
    oo,
    vv,
    x_pad,
    gathered,
    x_t,
    total,
    outgoing,
    incoming,
    scalars_out,
    scalars_in,
    norms_out,
    norms_in,
    halfway_a,
    halfway_b,
    coul_t,
    oo_t,
    load_sem,
    gather_send,
    gather_recv,
    sum_send,
    sum_recv,
    scalar_send,
    scalar_recv,
    norm_send,
    norm_recv,
):
    me = lax.axis_index("aux")
    n_trial, rows, n_virt = x_ref.shape
    aux_local, n_occ, _ = oo.shape
    width = x_pad.shape[1]
    half_trials = n_trial // 2
    half_cols = half_trials * n_occ
    lanes = 128
    f32, bf16 = jnp.float32, jnp.bfloat16

    loads = [
        pltpu.make_async_copy(source, target, load_sem.at[slot])
        for slot, (source, target) in enumerate(((oo_hbm, oo), (coul_hbm, coul), (vv_hbm, vv)))
    ]
    for load in loads:
        load.start()

    barrier = pltpu.get_barrier_semaphore()

    def greet(step, carry):
        pl.semaphore_signal(
            barrier, inc=1, device_id={"aux": lax.rem(me + step, n_dev)}, device_id_type=MESH
        )
        return carry

    lax.fori_loop(1, n_dev, greet, 0)

    x_pad[...] = jnp.zeros_like(x_pad)
    x_pad[:, :n_virt] = x_ref[...].reshape(n_trial * rows, n_virt)
    half_rows = half_trials * rows
    for half in range(2):
        gathered[half, me] = x_pad[half * half_rows : (half + 1) * half_rows].astype(bf16)
    pl.semaphore_wait(barrier, n_dev - 1)

    def to_peer(source, target, send_sem, recv_sem, step):
        return pltpu.make_async_remote_copy(
            src_ref=source,
            dst_ref=target,
            send_sem=send_sem.at[step],
            recv_sem=recv_sem.at[step],
            device_id={"aux": lax.rem(me + step, n_dev)},
            device_id_type=MESH,
        )

    pair = me + 1 - 2 * lax.rem(me, 2)
    chip_steps = sorted(range(2, n_dev, 2), key=lambda step: -min(step, n_dev - step))

    def block_copy(half, owner, peer, sem_at):
        return pltpu.make_async_remote_copy(
            src_ref=gathered.at[half, owner],
            dst_ref=gathered.at[half, owner],
            send_sem=gather_send.at[half, sem_at],
            recv_sem=gather_recv.at[half, sem_at],
            device_id={"aux": peer},
            device_id_type=MESH,
        )

    def pair_copy(half):
        return block_copy(half, me, pair, 1)

    def direct_copy(half, step):
        return block_copy(half, me, lax.rem(me + step, n_dev), step)

    def passed_copy(half, step):
        return block_copy(half, lax.rem(me + n_dev - step, n_dev), pair, step + 1)

    def pass_on(half):
        for step in reversed(chip_steps):
            direct_copy(half, step).wait_recv()
            passed_copy(half, step).start()

    def take_in(half):
        pair_copy(half).wait_recv()
        for step in reversed(chip_steps):
            passed_copy(half, step).wait_recv()
        wide = gathered[half].astype(f32).reshape(n_dev, half_trials, rows, width)
        for n in range(half_trials):
            at = half * half_trials + n
            x_t[:, at * n_occ : (at + 1) * n_occ] = wide[:, n].reshape(n_occ, width).T.astype(bf16)

    def sum_copy(half, step):
        peer = lax.rem(me + step, n_dev)
        return to_peer(
            outgoing.at[half, peer], incoming.at[half, me], sum_send.at[half], sum_recv.at[half], step
        )

    def scalar_copy(step):
        return to_peer(scalars_out, scalars_in.at[me], scalar_send, scalar_recv, step)

    def norm_copy(step):
        return to_peer(norms_out, norms_in.at[me], norm_send, norm_recv, step)

    def each(action):
        def body(step, carry):
            action(step)
            return carry

        lax.fori_loop(1, n_dev, body, 0)

    for half in range(2):
        for step in chip_steps:
            direct_copy(half, step).start()
        pair_copy(half).start()

    block = 16
    tiles = n_virt // block
    z_rows, z_cols = n_trial * block, aux_local * block
    loads[0].wait()

    def turn(index, carry):
        for p in range(group):
            at = index * group + p
            oo_t[pl.ds(at * n_occ, n_occ), :] = oo[at].T
        return carry

    lax.fori_loop(0, aux_local // group, turn, 0)
    loads[1].wait()
    loads[2].wait()
    pass_on(0)
    take_in(0)
    total[...] = jnp.zeros_like(total)

    def first_step(half, index, slot):
        slot[...] = jnp.dot(
            vv[pl.ds(index * group, group)].reshape(group * n_virt, n_virt),
            x_t[:n_virt, half * half_cols : (half + 1) * half_cols],
            preferred_element_type=f32,
        ).astype(bf16)

    def add_coulomb():
        left = jnp.concatenate(
            [
                jnp.concatenate(
                    [
                        x_t[t * block : (t + 1) * block, n * n_occ : (n + 1) * n_occ]
                        for n in range(n_trial)
                    ],
                    axis=0,
                )
                for t in range(tiles)
            ],
            axis=1,
        )
        z = jnp.dot(left, coul_t[...], preferred_element_type=f32)
        same = (
            lax.broadcasted_iota(jnp.int32, (z_rows, z_cols), 0) % block
            == lax.broadcasted_iota(jnp.int32, (z_rows, z_cols), 1) % block
        )
        z = jnp.sum(jnp.where(same, z, 0.0).reshape(n_trial, block, z_cols), axis=1)
        chunks = z_cols // lanes
        ones = (
            lax.broadcasted_iota(jnp.int32, (lanes, lanes), 0) // block
            == lax.broadcasted_iota(jnp.int32, (lanes, lanes), 1) // block
        ).astype(bf16)
        z = jnp.concatenate([z[:, c * lanes : (c + 1) * lanes] for c in range(chunks)], axis=0)
        coef = jnp.zeros_like(z)
        for _ in range(3):
            piece = z.astype(bf16)
            z = z - piece.astype(f32)
            coef = coef + jnp.dot(piece, ones, preferred_element_type=f32)
        coef = jnp.concatenate(
            [coef[c * n_trial : (c + 1) * n_trial] for c in range(chunks)], axis=1
        )
        coef = jnp.broadcast_to(coef[:, None, :], (n_trial, block, z_cols)).reshape(z_rows, z_cols)
        spread = jnp.where(same, coef, 0.0).astype(bf16)
        for index in range(tiles // 2):
            spans = [slice((2 * index + t) * block, (2 * index + t + 1) * block) for t in range(2)]
            right = jnp.concatenate(
                [coul[:, span, :].reshape(z_cols, n_occ) for span in spans], axis=1
            )
            part = 2.0 * jnp.dot(spread, right, preferred_element_type=f32)
            for t, span in enumerate(spans):
                for n in range(n_trial):
                    total[n, span, :] = (
                        total[n, span, :]
                        + part[n * block : (n + 1) * block, t * n_occ : (t + 1) * n_occ]
                    )

    first_step(0, 0, halfway_a)
    for half in range(2):

        def second_step(index, slot, half=half):
            left = jnp.concatenate(
                [
                    jnp.concatenate(
                        [
                            slot[p * n_virt : (p + 1) * n_virt, n * n_occ : (n + 1) * n_occ]
                            for p in range(group)
                        ],
                        axis=1,
                    )
                    for n in range(half_trials)
                ],
                axis=0,
            )
            right = oo_t[pl.ds(index * (group * n_occ), group * n_occ), :]
            part = jnp.dot(left, right, preferred_element_type=f32)
            for n in range(half_trials):
                at = half * half_trials + n
                total[at, :n_virt, :] = (
                    total[at, :n_virt, :] - part[n * n_virt : (n + 1) * n_virt, :]
                )

        def exchange(index, carry, half=half):
            first_step(half, 2 * index + 1, halfway_b)
            second_step(2 * index, halfway_a)
            first_step(half, 2 * index + 2, halfway_a)
            second_step(2 * index + 1, halfway_b)
            return carry

        groups = aux_local // group
        trips = groups // 2 - 1
        if half == 0:
            share = -(-tiles // trips)

            def exchange_and_turn(index, carry, exchange=exchange, share=share):
                for q in range(share):
                    t = jnp.minimum(index * share + q, tiles - 1)
                    coul_t[pl.ds(t * n_occ, n_occ), :] = (
                        coul[:, pl.ds(t * block, block), :].reshape(z_cols, n_occ).T
                    )
                return exchange(index, carry)

            middle = groups // 4
            lax.fori_loop(0, middle, exchange_and_turn, 0)
            pass_on(1)
            lax.fori_loop(middle, trips, exchange_and_turn, 0)
        else:
            lax.fori_loop(0, trips, exchange, 0)
        first_step(half, groups - 1, halfway_b)
        second_step(groups - 2, halfway_a)
        if half == 0:
            take_in(1)
            first_step(1, 0, halfway_a)
        second_step(groups - 1, halfway_b)
        if half == 0:
            add_coulomb()
        outgoing[half] = jnp.concatenate(
            [
                total[half * half_trials + n].T.reshape(n_dev, rows, width)
                for n in range(half_trials)
            ],
            axis=1,
        ).astype(bf16)
        each(lambda step, half=half: sum_copy(half, step).start())
        incoming[half, me] = outgoing[half, me]

    row_at = lax.broadcasted_iota(jnp.int32, (rows, n_occ), 0) + me * rows
    col_at = lax.broadcasted_iota(jnp.int32, (rows, n_occ), 1)
    occ_rows = jnp.sum(jnp.where(row_at == col_at, occ_ref[...], 0.0), axis=1, keepdims=True)
    diagonal = vir_ref[...] - occ_rows

    def whole(value):
        return jnp.sum(jnp.sum(value, axis=0, keepdims=True), axis=1, keepdims=True)

    numer, denom = [], []
    for n in range(n_trial):
        own = x_ref[n]
        square = own * own
        x_n = x_t[:, n * n_occ : (n + 1) * n_occ].astype(f32)
        numer.append(whole(x_n * total[n]) + whole(diagonal * square))
        denom.append(whole(square))
    for n in range(n_trial):
        scalars_out[n : n + 1, :] = jnp.broadcast_to(numer[n], (1, lanes))
        scalars_out[n_trial + n : n_trial + n + 1, :] = jnp.broadcast_to(denom[n], (1, lanes))
    each(lambda step: scalar_copy(step).start())
    scalars_in[me] = scalars_out[...]

    for half in range(2):
        each(lambda step, half=half: sum_copy(half, step).wait_recv())
    each(lambda step: scalar_copy(step).wait_recv())

    sums = jnp.sum(scalars_in[...], axis=0)
    precond = []
    for n in range(n_trial):
        if n % half_trials == 0:
            summed = jnp.sum(incoming[n // half_trials].astype(f32), axis=0)
        at = (n % half_trials) * rows
        own = x_ref[n]
        sigma = diagonal * own + summed[at : at + rows, :n_virt]
        sigma_ref[n] = sigma
        omega = sums[n : n + 1, :1] / (sums[n_trial + n : n_trial + n + 1, :1] + 1e-06)
        resid = sigma - omega * own
        precond.append(resid / jnp.maximum(jnp.abs(diagonal - omega), 1.0))
        norms_out[n : n + 1, :] = jnp.broadcast_to(whole(precond[n] * precond[n]), (1, lanes))
    each(lambda step: norm_copy(step).start())
    norms_in[me] = norms_out[...]
    each(lambda step: norm_copy(step).wait_recv())
    norms = jnp.sum(norms_in[...], axis=0)
    count = float(n_occ * n_virt)
    for n in range(n_trial):
        update_ref[n] = precond[n] * lax.rsqrt(norms[n : n + 1, :1] / count + 1e-06)

    for half in range(2):
        pair_copy(half).wait_send()
        for step in chip_steps:
            direct_copy(half, step).wait_send()
            passed_copy(half, step).wait_send()
    for half in range(2):
        each(lambda step, half=half: sum_copy(half, step).wait_send())
    each(lambda step: scalar_copy(step).wait_send())
    each(lambda step: norm_copy(step).wait_send())


def hand_over(sigma_in, update_in, sigma_ref, update_ref):
    sigma_ref[...] = sigma_in[...]
    update_ref[...] = update_in[...]


def on_device(n_dev, trial_vecs, occ_energy, vir_energy, coul_ov, exch_oo, exch_vv):
    n_trial, rows, n_virt = trial_vecs.shape
    aux_local, n_occ, _ = exch_oo.shape
    width = -(-n_virt // 128) * 128
    half_rows = n_trial // 2 * rows
    group = math.gcd(aux_local // 2, 4)
    vmem = pl.BlockSpec(memory_space=pltpu.VMEM)
    anywhere = pl.BlockSpec(memory_space=pl.ANY)
    out = jax.ShapeDtypeStruct(trial_vecs.shape, jnp.float32)
    dma = pltpu.SemaphoreType.DMA
    sigma, update = pl.pallas_call(
        functools.partial(sigma_kernel, n_dev, group),
        out_shape=(out, out),
        in_specs=[vmem] * 3 + [anywhere] * 3,
        out_specs=(vmem, vmem),
        scratch_shapes=[
            pltpu.VMEM((aux_local, n_virt, n_occ), jnp.bfloat16),
            pltpu.VMEM((aux_local, n_occ, n_occ), jnp.bfloat16),
            pltpu.VMEM((aux_local, n_virt, n_virt), jnp.bfloat16),
            pltpu.VMEM((n_trial * rows, width), jnp.float32),
            pltpu.VMEM((2, n_dev, half_rows, width), jnp.bfloat16),
            pltpu.VMEM((width, n_trial * n_occ), jnp.bfloat16),
            pltpu.VMEM((n_trial, width, n_occ), jnp.float32),
            pltpu.VMEM((2, n_dev, half_rows, width), jnp.bfloat16),
            pltpu.VMEM((2, n_dev, half_rows, width), jnp.bfloat16),
            pltpu.VMEM((2 * n_trial, 128), jnp.float32),
            pltpu.VMEM((n_dev, 2 * n_trial, 128), jnp.float32),
            pltpu.VMEM((2 * n_trial, 128), jnp.float32),
            pltpu.VMEM((n_dev, 2 * n_trial, 128), jnp.float32),
            pltpu.VMEM((group * n_virt, n_trial // 2 * n_occ), jnp.bfloat16),
            pltpu.VMEM((group * n_virt, n_trial // 2 * n_occ), jnp.bfloat16),
            pltpu.VMEM((n_virt * n_occ // 16, aux_local * 16), jnp.bfloat16),
            pltpu.VMEM((aux_local * n_occ, n_occ), jnp.bfloat16),
            dma((3,)),
            dma((2, n_dev)),
            dma((2, n_dev)),
            dma((2, n_dev)),
            dma((2, n_dev)),
            dma((n_dev,)),
            dma((n_dev,)),
            dma((n_dev,)),
            dma((n_dev,)),
        ],
        compiler_params=pltpu.CompilerParams(
            collective_id=0, has_side_effects=True, vmem_limit_bytes=56 * 1024 * 1024
        ),
    )(
        trial_vecs,
        occ_energy[None, :],
        vir_energy[None, :],
        coul_ov.transpose(0, 2, 1),
        exch_oo,
        exch_vv,
    )
    return pl.pallas_call(
        hand_over, out_shape=(out, out), in_specs=[vmem] * 2, out_specs=(vmem, vmem)
    )(sigma, update)


def contract(rows_x, coul_ov, exch_oo, exch_vv):
    aux_coef = jnp.einsum("pia,nia->np", coul_ov, rows_x, preferred_element_type=jnp.float32)
    coulomb = jnp.einsum(
        "pia,np->nia", coul_ov, aux_coef.astype(jnp.bfloat16), preferred_element_type=jnp.float32
    )
    aux_local, n_occ, _ = exch_oo.shape
    n_virt = exch_vv.shape[1]
    group_size = math.gcd(aux_local, 16)
    vv_groups = exch_vv.reshape(aux_local // group_size, group_size, n_virt, n_virt)
    oo_groups = exch_oo.reshape(aux_local // group_size, group_size, n_occ, n_occ)

    def advance(running, parts_pair):
        vv_part, oo_part = parts_pair
        halfway = jnp.einsum(
            "pab,njb->pnja", vv_part, rows_x, preferred_element_type=jnp.float32
        ).astype(jnp.bfloat16)
        return (
            running
            + jnp.einsum("pij,pnja->nia", oo_part, halfway, preferred_element_type=jnp.float32),
            None,
        )

    exchange, _ = lax.scan(advance, jnp.zeros(rows_x.shape, jnp.float32), (vv_groups, oo_groups))
    return 2.0 * coulomb - exchange


def on_device_plain(trial_vecs, occ_energy, vir_energy, coul_ov, exch_oo, exch_vv):
    local_rows = trial_vecs.shape[1]
    n_occ, n_virt = coul_ov.shape[1:]
    row_start = lax.axis_index("aux") * local_rows
    rows_x = lax.all_gather(trial_vecs.astype(jnp.bfloat16), "aux", axis=1, tiled=True)
    summed = lax.psum_scatter(
        contract(rows_x, coul_ov, exch_oo, exch_vv), "aux", scatter_dimension=1, tiled=True
    )
    occ_rows = lax.dynamic_slice_in_dim(occ_energy, row_start, local_rows, 0)
    diagonal = vir_energy[None, :] - occ_rows[:, None]
    sigma = diagonal[None] * trial_vecs + summed
    sums = lax.psum(
        jnp.stack([jnp.sum(trial_vecs * sigma, (1, 2)), jnp.sum(trial_vecs * trial_vecs, (1, 2))]),
        "aux",
    )
    omega = (sums[0] / (sums[1] + 1e-06))[:, None, None]
    precond = (sigma - omega * trial_vecs) / jnp.maximum(jnp.abs(diagonal[None] - omega), 1.0)
    squares = lax.psum(jnp.sum(precond * precond, axis=(1, 2)), "aux") / (n_occ * n_virt)
    return sigma, precond * lax.rsqrt(squares + 1e-06)[:, None, None]


def solution(mesh):
    n_dev = mesh.shape["aux"]

    def body(trial_vecs, occ_energy, vir_energy, coul_ov, exch_oo, exch_vv):
        n_trial, rows, n_virt = trial_vecs.shape
        aux_local, n_occ, _ = exch_oo.shape
        tiled = (
            n_trial % 4 == 0
            and rows % 8 == 0
            and n_occ % 128 == 0
            and n_virt % 32 == 0
            and aux_local % 16 == 0
            and aux_local >= 32
            and n_dev % 2 == 0
        )
        args = (trial_vecs, occ_energy, vir_energy, coul_ov, exch_oo, exch_vv)
        return on_device(n_dev, *args) if tiled else on_device_plain(*args)

    in_specs = (
        P("geom", "aux", None),
        P("geom"),
        P("geom"),
        P(("geom", "aux"), None, None),
        P(("geom", "aux"), None, None),
        P(("geom", "aux"), None, None),
    )
    out_specs = (P("geom", "aux", None), P("geom", "aux", None))
    return jax.shard_map(body, mesh=mesh, in_specs=in_specs, out_specs=out_specs, check_vma=False)
```
